128 devices in a mesh: smp: 16 (over x_hi, z, core), feat: 8 (over y, x_lo).
Axes of the slice: x: 4 (x_hi: 2, x_lo: 2; x = x_hi * 2 + x_lo), y: 4, z: 4, core: 2. Of those that a mesh axis runs over, the one named last changes fastest.
Arguments:
- design: bfloat16 [16384, 16384], P('smp', 'feat'), may hold values from -0.125 to 0.125
- targets: float32 [16384, 256], P('smp'), may hold values from -6 to 6
- sample_weight: float32 [16384], P('smp'), may hold values from 0.3 to 3
- penalty: float32 [16384], P('feat'), may hold values from 4 to 40
- coef: float32 [16384, 256], P('feat'), may hold values from -6 to 6
- coef_dual: float32 [16384, 256], P('feat'), may hold values from -4 to 4
- tile_coef_dual: float32 [16, 16384, 256], P('smp', 'feat'), may hold values from -4 to 4
- fit: float32 [16384, 256], P('smp'), may hold values from -6 to 6
- fit_dual: float32 [16384, 256], P('smp'), may hold values from -4 to 4
- tile_fit: float32 [8, 16384, 256], P('feat', 'smp'), may hold values from -6 to 6
- tile_fit_dual: float32 [8, 16384, 256], P('feat', 'smp'), may hold values from -4 to 4
Outputs:
- coef_out: float32 [16384, 256], P('feat')
- fit_out: float32 [16384, 256], P('smp')
The draws below stay inside these ranges and needn't reach their ends.
All inputs are finite; a program needn't handle non-finite values.
Results may differ from the reference program's by a relative error of at most 0.0027.
Values sent between devices are 32-bit elements; how exact they have to be, the bound alone decides.
A program may use at most 128 MiB of HBM per device.

```python
import math
import jax
import jax.numpy as jnp
from jax import lax

FEATURES = 16384
OUTPUTS = 256
ROWS_DEV = 1024
ITERS = 2
SAMPLES = 16384
N_SMP = 16
N_FEAT = 8


def level_of(stream_key, shape, pieces, smallest, top_value):
    loudness = 1.0
    for position, shards_of in pieces:
        heights = jax.random.uniform(jax.random.fold_in(jax.random.fold_in(stream_key, 6), position), (shards_of,), jnp.float32, smallest / len(pieces), top_value / len(pieces))
        loudness = loudness * jnp.repeat(jnp.exp(heights), shape[position] // shards_of).reshape((-1,) + (1,) * (len(shape) - 1 - position))
    return loudness


def normal_values(stream_key, dims, spread, bound, cuts=(), held_as=jnp.bfloat16):
    level = level_of(stream_key, dims, cuts, -0.22, 0.18) if cuts else 1.0
    values = jax.random.normal(stream_key, dims, jnp.float32) * spread * level
    return jnp.minimum(jnp.maximum(values, -bound), bound).astype(held_as)


def setup_inputs(seed: int = 0) -> dict:
    seeds = jax.random.split(jax.random.key(seed), 12)
    design = normal_values(seeds[0], (SAMPLES, FEATURES), (FEATURES // N_FEAT) ** -0.5, 0.125, ((0, 16), (1, 8)))
    targets = normal_values(seeds[1], (SAMPLES, OUTPUTS), 1.0, 6.0, ((0, 16),), jnp.float32)
    sample_weight = jnp.clip(jnp.exp(math.log(3.0) - 2.3025851 * jax.random.uniform(seeds[2], (SAMPLES,), jnp.float32) ** level_of(seeds[2], (SAMPLES,), ((0, 16),), -0.2, 0.2)), 0.3, 3.0)
    penalty = jnp.clip(jnp.exp(math.log(40.0) - 2.3025851 * jax.random.uniform(seeds[3], (FEATURES,), jnp.float32) ** level_of(seeds[3], (FEATURES,), ((0, 8),), -0.2, 0.2)), 4.0, 40.0)
    coef = normal_values(seeds[4], (FEATURES, OUTPUTS), 1.0, 6.0, ((0, 8),), jnp.float32)
    coef_dual = normal_values(seeds[5], (FEATURES, OUTPUTS), 0.5, 4.0, ((0, 8),), jnp.float32)
    tile_coef_dual = normal_values(seeds[6], (N_SMP, FEATURES, OUTPUTS), 0.5, 4.0, ((0, 16), (1, 8)), jnp.float32)
    fit = normal_values(seeds[7], (SAMPLES, OUTPUTS), 1.0, 6.0, ((0, 16),), jnp.float32)
    fit_dual = normal_values(seeds[8], (SAMPLES, OUTPUTS), 0.5, 4.0, ((0, 16),), jnp.float32)
    tile_fit = normal_values(seeds[9], (N_FEAT, SAMPLES, OUTPUTS), 1.0, 6.0, ((0, 8), (1, 16)), jnp.float32)
    tile_fit_dual = normal_values(seeds[10], (N_FEAT, SAMPLES, OUTPUTS), 0.5, 4.0, ((0, 8), (1, 16)), jnp.float32)
    return {"design": design, "targets": targets, "sample_weight": sample_weight, "penalty": penalty, "coef": coef, "coef_dual": coef_dual, "tile_coef_dual": tile_coef_dual, "fit": fit, "fit_dual": fit_dual, "tile_fit": tile_fit, "tile_fit_dual": tile_fit_dual}


def shrink_rows(values, penalty):
    norms = jnp.sqrt(lax.optimization_barrier(jnp.sum(values * values, axis=1)) + 1e-06)
    return values * (jnp.maximum(norms - penalty, 0.0) / norms)[:, None]

def reference(design, targets, sample_weight, penalty, coef, coef_dual, tile_coef_dual, fit, fit_dual, tile_fit, tile_fit_dual):
    rows = ROWS_DEV
    cols = FEATURES // N_FEAT
    count = N_SMP * N_FEAT
    zero = jnp.int32(0)
    tiles = jnp.arange(count, dtype=jnp.int32)

    def block(t):
        i = t // N_FEAT
        j = t % N_FEAT
        return lax.dynamic_slice(design, (i * rows, j * cols), (rows, cols))

    def factor(t):
        tile = block(t)
        gram = lax.dot_general(tile.astype(jnp.float32), tile.astype(jnp.float32), (((1,), (1,)), ((), ())), preferred_element_type=jnp.float32)
        return jnp.linalg.cholesky(gram + jnp.eye(rows, dtype=jnp.float32))
    factors = lax.map(factor, tiles)
    weight = sample_weight[:, None]
    for step in range(ITERS):
        fit_half = (fit - fit_dual + weight * targets) / (1.0 + weight)
        coef_half = shrink_rows(coef - coef_dual, penalty[:, None][:, 0])

        def project(t):
            i = t // N_FEAT
            j = t % N_FEAT
            tile = block(t)
            lower = factors[t]
            local = lax.dynamic_slice(coef, (j * cols, zero), (cols, OUTPUTS)) - lax.dynamic_slice(tile_coef_dual, (i, j * cols, zero), (1, cols, OUTPUTS))[0]
            target = lax.dynamic_slice(tile_fit, (j, i * rows, zero), (1, rows, OUTPUTS))[0] - lax.dynamic_slice(tile_fit_dual, (j, i * rows, zero), (1, rows, OUTPUTS))[0]
            resid = jnp.dot(tile.astype(jnp.float32), local.astype(jnp.bfloat16).astype(jnp.float32), preferred_element_type=jnp.float32) - target
            solved = jax.scipy.linalg.cho_solve((lower, True), resid)
            back = lax.dot_general(tile.astype(jnp.float32), solved.astype(jnp.bfloat16).astype(jnp.float32), (((0,), (0,)), ((), ())), preferred_element_type=jnp.float32)
            tile_coef = local - back
            tile_out = jnp.dot(tile.astype(jnp.float32), tile_coef.astype(jnp.bfloat16).astype(jnp.float32), preferred_element_type=jnp.float32)
            return (tile_coef, tile_out)
        tile_coef_half, tile_fit_half = lax.map(project, tiles)
        coef_parts = tile_coef_half.reshape(N_SMP, N_FEAT, cols, OUTPUTS)
        fit_parts = tile_fit_half.reshape(N_SMP, N_FEAT, rows, OUTPUTS)
        coef_total = lax.optimization_barrier(jnp.sum(coef_parts, axis=0)).reshape(FEATURES, OUTPUTS)
        coef_new = (coef_half + coef_total) / (N_SMP + 1.0)
        fit_total = lax.optimization_barrier(jnp.sum(fit_parts, axis=1)).reshape(SAMPLES, OUTPUTS)
        gap = (fit_half - fit_total) / (N_FEAT + 1.0)
        fit_new = fit_half - gap
        tile_fit_full = jnp.transpose(fit_parts, (1, 0, 2, 3)).reshape(N_FEAT, SAMPLES, OUTPUTS)
        tile_fit_new = tile_fit_full + gap[None]
        tile_coef_full = coef_parts.reshape(N_SMP, FEATURES, OUTPUTS)
        coef_dual = coef_dual + coef_half - coef_new
        fit_dual = fit_dual + fit_half - fit_new
        tile_coef_dual = tile_coef_dual + tile_coef_full - coef_new[None]
        tile_fit_dual = tile_fit_dual + tile_fit_full - tile_fit_new
        coef = coef_new
        fit = fit_new
        tile_fit = tile_fit_new
    return (coef, fit)
```

```python
import functools
import jax
import jax.numpy as jnp
from jax import lax
from jax.experimental import pallas as pl
from jax.experimental.pallas import tpu as pltpu
from jax.sharding import PartitionSpec as P

F32, BF16 = jnp.float32, jnp.bfloat16
B = 128


def recip(x):
    y = pl.reciprocal(x, approx=True)
    y = y * (2.0 - x * y)
    return y * (2.0 - x * y)


def small_inverse(e, n):
    e = {(i, j): e[i][j] for i in range(n) for j in range(i, n)}
    at = lambda i, j: e[(i, j) if i <= j else (j, i)]
    for p in range(n):
        r = recip(e[p, p])
        w = {i: at(i, p) * r for i in range(n) if i != p}
        new = {}
        for i in range(n):
            for j in range(i, n):
                if i == p and j == p:
                    new[i, j] = -r
                elif i == p or j == p:
                    o = j if i == p else i
                    new[i, j] = w[o]
                else:
                    new[i, j] = e[i, j] - at(i, p) * w[j]
        e = new
    return [[-at(i, j) for j in range(n)] for i in range(n)]


def sweep128(block):
    rows = [block[8 * b : 8 * b + 8, :] for b in range(16)]
    lane = lax.broadcasted_iota(jnp.int32, (8, B), 1)
    sub = lax.broadcasted_iota(jnp.int32, (8, B), 0)
    for g in range(16):
        here = (lane >= 8 * g) & (lane < 8 * g + 8)
        cols = [
            [jnp.broadcast_to(rows[b][:, 8 * g + j : 8 * g + j + 1], (8, B)) for j in range(8)]
            for b in range(16)
        ]
        e = [[jnp.broadcast_to(cols[g][j][i : i + 1, :], (8, B)) for j in range(8)] for i in range(8)]
        q = small_inverse(e, 8)
        r = [
            jnp.where(
                here,
                jnp.where(lane == 8 * g + j, -1.0, 0.0),
                jnp.broadcast_to(rows[g][j : j + 1, :], (8, B)),
            )
            for j in range(8)
        ]
        w = []
        for i in range(8):
            t = [q[i][j] * r[j] for j in range(8)]
            while len(t) > 1:
                t = [t[a] + t[a + 1] for a in range(0, len(t), 2)]
            w.append(t[0])
        order = [(g + 1 + b) % 16 for b in range(16)]
        for b in order:
            if b == g:
                out = w[0]
                for i in range(1, 8):
                    out = jnp.where(sub == i, w[i], out)
                rows[b] = out
            else:
                t = [cols[b][j] * w[j] for j in range(8)]
                while len(t) > 1:
                    t = [t[a] + t[a + 1] for a in range(0, len(t), 2)]
                rows[b] = jnp.where(here, 0.0, rows[b]) - t[0]
    return jnp.concatenate(rows, axis=0)


def split(x):
    hi = x.astype(BF16)
    return hi, (x - hi.astype(F32)).astype(BF16)


def left(x):
    hi, lo = split(x)
    return jnp.concatenate([hi, lo, hi, lo], axis=1)


def right(x):
    hi, lo = split(x)
    return jnp.concatenate([hi, hi, lo, lo], axis=0)


def dot(a, b):
    return jnp.dot(a, b, preferred_element_type=F32)


def factor_kernel(n, a_ref, hi_ref, lo_ref, g, panel):
    R = 256
    for i in range(n // R):
        g[pl.ds(i * R, R), :] = lax.dot_general(
            a_ref[pl.ds(i * R, R), :], a_ref[...], (((1,), (1,)), ((), ())), preferred_element_type=F32
        )
    eye = jnp.where(
        lax.broadcasted_iota(jnp.int32, (B, B), 0) == lax.broadcasted_iota(jnp.int32, (B, B), 1), 1.0, 0.0
    )
    for k in range(n // B):
        at = pl.ds(k * B, B)
        g[at, at] = g[at, at] + eye

    def step(k, _):
        at = pl.ds(pl.multiple_of(k * B, B), B)
        neg = sweep128(g[at, at])
        panel[...] = left(g[:, at])
        w = dot(left(-neg), right(g[at, :]))
        g[at, :] = w
        g[:, at] = jnp.zeros((n, B), F32)
        g[at, at] = neg
        w = right(g[at, :])
        for i in range(n // R):
            rows = pl.ds(i * R, R)
            g[rows, :] = g[rows, :] - dot(panel[rows, :], w)
        g[at, :] = g[at, :] * 0.0 + (w[:B].astype(F32) + w[2 * B : 3 * B].astype(F32))
        return 0

    lax.fori_loop(0, n // B, step, 0)
    for i in range(n // R):
        rows = pl.ds(i * R, R)
        hi_ref[rows, :], lo_ref[rows, :] = split(-g[rows, :])


def factor(a):
    n = a.shape[0]
    return pl.pallas_call(
        functools.partial(factor_kernel, n),
        out_shape=[jax.ShapeDtypeStruct((n, n), BF16)] * 2,
        in_specs=[pl.BlockSpec(memory_space=pltpu.VMEM)],
        out_specs=[pl.BlockSpec(memory_space=pltpu.VMEM)] * 2,
        scratch_shapes=[pltpu.VMEM((n, n), F32), pltpu.VMEM((n, 4 * B), BF16)],
        compiler_params=pltpu.CompilerParams(vmem_limit_bytes=56 * 2**20),
    )(a)


ITERS = 2
MESH = pl.DeviceIdType.MESH
SUBS = 2
VMEM_LIMIT = 60 * 2**20


def shrink_rows(values, penalty):
    norms = jnp.sqrt(jnp.sum(values * values, axis=1, keepdims=True) + 1e-06)
    return values * (jnp.maximum(norms - penalty, 0.0) / norms)


def column(row):
    return jnp.transpose(jnp.broadcast_to(row, (B, B)))[:, :1]


def iterate_kernel(
    design_hbm, hi_hbm, lo_hbm, targets_hbm, weight_ref, penalty_ref, coef_hbm, coef_dual_hbm,
    tile_dual_hbm, fit_hbm, fit_dual_hbm, part_hbm, part_dual_hbm,
    coef_out, fit_out,
    design, hi, lo, coef, coef_dual, tile_dual, fit, fit_dual, targets, part, part_dual,
    mine, from_core, from_z, to_x, from_x, whole, outs, from_y, to_xl, from_xl, gaps,
    load_sem, send_sem, recv_sem, store_sem,
):
    rows, cols = design.shape
    width = coef.shape[1]
    smp, feat = lax.axis_index("smp"), lax.axis_index("feat")
    xh, z, c = smp // 8, (smp // 2) % 4, smp % 2
    y, xl = feat // 2, feat % 2
    core_peer = (smp + 1 - 2 * c, feat)
    z_peer = [None] + [(xh * 8 + ((z + o) % 4) * 2 + c, feat) for o in (1, 2, 3)]
    x_peer = ((smp + 8) % 16, feat)
    y_peer = [None] + [(smp, ((y + o) % 4) * 2 + xl) for o in (1, 2, 3)]
    xl_peer = (smp, feat + 1 - 2 * xl)
    peers = [core_peer, x_peer, xl_peer] + z_peer[1:] + y_peer[1:]
    barrier = pltpu.get_barrier_semaphore()
    for peer in peers:
        pl.semaphore_signal(barrier, inc=1, device_id=peer, device_id_type=MESH)

    seg = cols // SUBS // 8
    half = 4 * seg
    quarter = rows // 4

    def at(u, h, q):
        return pl.multiple_of(u * 8 * seg + h * half + q * seg, seg)

    def own_fit(q):
        return pl.ds(pl.multiple_of(q * quarter, quarter), quarter)

    loads = []

    def load(src, dst):
        copy = pltpu.make_async_copy(src, dst, load_sem.at[len(loads)])
        copy.start()
        loads.append(copy)
        return copy

    l_coef = load(coef_hbm, coef)
    l_tile_dual = load(tile_dual_hbm, tile_dual)
    l_part = load(part_hbm, part)
    l_part_dual = load(part_dual_hbm, part_dual)
    l_design = load(design_hbm, design)
    l_hi = load(hi_hbm, hi)
    l_lo = load(lo_hbm, lo)
    l_own = []
    for u in range(SUBS):
        mine_rows = pl.ds(at(u, c, z), seg)
        l_own.append(load(coef_dual_hbm.at[mine_rows], coef_dual.at[u]))
    l_fit = [
        load(src.at[own_fit(y)], dst)
        for src, dst in ((fit_hbm, fit), (fit_dual_hbm, fit_dual), (targets_hbm, targets))
    ]

    count = [0]
    sends = []

    def send(src, dst, peer):
        i = count[0]
        count[0] += 1
        copy = pltpu.make_async_remote_copy(
            src_ref=src, dst_ref=dst, send_sem=send_sem.at[i], recv_sem=recv_sem.at[i],
            device_id=peer, device_id_type=MESH,
        )
        copy.start()
        sends.append(copy)
        return copy

    for copy in (l_coef, l_tile_dual):
        copy.wait()
    own_coef = [coef[pl.ds(at(u, c, z), seg), :] for u in range(SUBS)]
    coef[...] = coef[...] - tile_dual[...]
    for copy in (l_part, l_part_dual, l_design):
        copy.wait()
    part[...] = part[...] - part_dual[...]
    M = 512
    for m in range(rows // M):
        ms = pl.ds(m * M, M)
        part[ms, :] = dot(design[ms, :], coef[...].astype(BF16)) - part[ms, :]
    for copy in l_own + l_fit + [l_hi, l_lo]:
        copy.wait()
    weight = jnp.concatenate(
        [column(weight_ref[pl.ds(y * (quarter // B) + i, 1), :]) for i in range(quarter // B)], axis=0
    )
    penalty = [column(penalty_ref[pl.ds(at(u, c, z) // B, 1), :]) for u in range(SUBS)]
    own_dual = [coef_dual[u] for u in range(SUBS)]
    pl.semaphore_wait(barrier, len(peers))
    stores = []

    def store(src, dst):
        copy = pltpu.make_async_copy(src, dst, store_sem.at[len(stores)])
        copy.start()
        stores.append(copy)

    for it in range(ITERS):
        last = it == ITERS - 1
        r_hi, r_lo = split(part[...])
        solved = dot(hi[...], r_hi) + dot(lo[...], r_hi) + dot(hi[...], r_lo)
        sb = solved.astype(BF16)
        cores = []
        N = cols // SUBS
        for u in range(SUBS):
            us = pl.ds(u * N, N)
            back = lax.dot_general(
                design[:, u * N : (u + 1) * N], sb, (((0,), (0,)), ((), ())), preferred_element_type=F32
            )
            tile = coef[us, :] - back
            mine[it, us, :] = tile
            cores.append(
                send(mine.at[it, pl.ds(at(u, 1 - c, 0), half)], from_core.at[it, u], core_peer)
            )
        tb = mine[it].astype(BF16)
        if not last:
            tile_dual[...] = tile_dual[...] + mine[it]
        rz = [None] * SUBS

        def to_z(u):
            cores[u].wait_recv()
            here = pl.ds(at(u, c, 0), half)
            mine[it, here, :] = mine[it, here, :] + from_core[it, u]
            rz[u] = [
                send(mine.at[it, pl.ds(at(u, c, (z + o) % 4), seg)], from_z.at[it, u, o - 1], z_peer[o])
                for o in (2, 1, 3)
            ]

        to_z(0)
        for m in range(rows // M):
            ms = pl.ds(m * M, M)
            outs[it, ms, :] = dot(design[ms, :], tb)
            if m + 1 < SUBS:
                to_z(m + 1)
        ry = [send(outs.at[it, own_fit((y + o) % 4)], from_y.at[it, o - 1], y_peer[o]) for o in (2, 1, 3)]
        coef_half = [shrink_rows(own_coef[u] - own_dual[u], penalty[u]) for u in range(SUBS)]
        fit_half = (fit[...] - fit_dual[...] + weight * targets[...]) / (1.0 + weight)
        if not last:
            part_dual[...] = part_dual[...] + outs[it]
        rx = []
        for u in range(SUBS):
            for copy in rz[u]:
                copy.wait_recv()
            here = pl.ds(at(u, c, z), seg)
            to_x[it, u] = (mine[it, here, :] + from_z[it, u, 0]) + (from_z[it, u, 1] + from_z[it, u, 2])
            rx.append(send(to_x.at[it, u], from_x.at[it, u], x_peer))
        for copy in ry:
            copy.wait_recv()
        to_xl[it] = (outs[it, own_fit(y), :] + from_y[it, 0]) + (from_y[it, 1] + from_y[it, 2])
        rxl = send(to_xl.at[it], from_xl.at[it], xl_peer)
        gz, gc = [], []
        for u in range(SUBS):
            rx[u].wait_recv()
            new = (coef_half[u] + (to_x[it, u] + from_x[it, u])) / 17.0
            here = pl.ds(at(u, c, z), seg)
            whole[it, here, :] = new
            gz.append([send(whole.at[it, here], whole.at[it, here], z_peer[o]) for o in (2, 1, 3)])
            gc.append([send(whole.at[it, here], whole.at[it, here], core_peer)])
            own_dual[u] = own_dual[u] + coef_half[u] - new
            own_coef[u] = new
        rxl.wait_recv()
        gap = (fit_half - (to_xl[it] + from_xl[it])) / 9.0
        fit_new = fit_half - gap
        gaps[it, own_fit(y), :] = fit_new if last else gap
        gy = [send(gaps.at[it, own_fit(y)], gaps.at[it, own_fit(y)], y_peer[o]) for o in (2, 1, 3)]
        if not last:
            fit_dual[...] = fit_dual[...] + fit_half - fit_new
            fit[...] = fit_new
        for u in range(SUBS):
            for o, copy in zip((2, 1, 3), gz[u]):
                copy.wait_recv()
                there = pl.ds(at(u, c, (z + 4 - o) % 4), seg)
                gc[u].append(send(whole.at[it, there], whole.at[it, there], core_peer))
        for copy in gy:
            copy.wait_recv()
        if last:
            store(gaps.at[it], fit_out)
        else:
            total = gaps[it] + outs[it]
            part[...] = total - (part_dual[...] - total)
        for u in range(SUBS):
            us = pl.ds(u * N, N)
            for copy in gc[u]:
                copy.wait_recv()
            if last:
                store(whole.at[it, us], coef_out.at[us])
            else:
                new = whole[it, us, :]
                local = new - (tile_dual[us, :] - new)
                coef[us, :] = local
                lb = local.astype(BF16)
                for m in range(rows // M):
                    ms = pl.ds(m * M, M)
                    prod = dot(design[ms, u * N : (u + 1) * N], lb)
                    part[ms, :] = prod - part[ms, :] if u == 0 else prod + part[ms, :]
    for copy in sends:
        copy.wait_send()
    for copy in stores:
        copy.wait()


def iterate(design, hi, lo, targets, weight, penalty, coef, coef_dual, tile_dual, fit, fit_dual, part, part_dual):
    rows, cols = design.shape
    width = coef.shape[1]
    seg = cols // SUBS // 8
    quarter = rows // 4
    any_ = pl.BlockSpec(memory_space=pl.ANY)
    vmem = pl.BlockSpec(memory_space=pltpu.VMEM)
    f32 = lambda *shape: pltpu.VMEM(shape, F32)
    wide = lambda r: f32(r, width)
    n_copies = ITERS * (14 * SUBS + 7 + 2 * SUBS)
    return pl.pallas_call(
        iterate_kernel,
        out_shape=[jax.ShapeDtypeStruct((cols, width), F32), jax.ShapeDtypeStruct((rows, width), F32)],
        in_specs=[any_] * 4 + [vmem] * 2 + [any_] * 7,
        out_specs=[any_] * 2,
        scratch_shapes=[
            pltpu.VMEM((rows, cols), BF16), pltpu.VMEM((rows, rows), BF16), pltpu.VMEM((rows, rows), BF16),
            wide(cols), f32(SUBS, seg, width), wide(cols), wide(quarter), wide(quarter), wide(quarter),
            wide(rows), wide(rows),
            f32(ITERS, cols, width), f32(ITERS, SUBS, 4 * seg, width), f32(ITERS, SUBS, 3, seg, width),
            f32(ITERS, SUBS, seg, width), f32(ITERS, SUBS, seg, width), f32(ITERS, cols, width),
            f32(ITERS, rows, width), f32(ITERS, 3, quarter, width), f32(ITERS, quarter, width),
            f32(ITERS, quarter, width), f32(ITERS, rows, width),
            pltpu.SemaphoreType.DMA((10 + SUBS,)), pltpu.SemaphoreType.DMA((n_copies,)),
            pltpu.SemaphoreType.DMA((n_copies,)), pltpu.SemaphoreType.DMA((SUBS + 1,)),
        ],
        compiler_params=pltpu.CompilerParams(
            collective_id=0, has_side_effects=True, vmem_limit_bytes=VMEM_LIMIT
        ),
    )(design, hi, lo, targets, weight.reshape(-1, B), penalty.reshape(-1, B), coef, coef_dual, tile_dual, fit,
      fit_dual, part, part_dual)


def per_device(design, targets, weight, penalty, coef, coef_dual, tile_dual, fit, fit_dual, part, part_dual):
    hi, lo = factor(design)
    return tuple(iterate(design, hi, lo, targets, weight, penalty, coef, coef_dual, tile_dual[0], fit, fit_dual,
                   part[0], part_dual[0]))


def solution(mesh):
    return jax.shard_map(
        per_device,
        mesh=mesh,
        in_specs=(
            P("smp", "feat"),
            P("smp", None),
            P("smp"),
            P("feat"),
            P("feat", None),
            P("feat", None),
            P("smp", "feat", None),
            P("smp", None),
            P("smp", None),
            P("feat", "smp", None),
            P("feat", "smp", None),
        ),
        out_specs=(P("feat", None), P("smp", None)),
        check_vma=False,
    )
```

```python
import functools
import jax
import jax.numpy as jnp
from jax import lax
from jax.experimental import pallas as pl
from jax.experimental.pallas import tpu as pltpu
from jax.sharding import PartitionSpec as P

F32, BF16 = jnp.float32, jnp.bfloat16
B = 128
NN, NT, TN = ((1,), (0,)), ((1,), (1,)), ((0,), (0,))


def split(x):
    hi = x.astype(BF16)
    return hi, (x - hi.astype(F32)).astype(BF16)


def dot(a, b, dims=NN):
    return lax.dot_general(a, b, (dims, ((), ())), preferred_element_type=F32)


def dot3(a, b, dims=NN):
    left = jnp.concatenate([a[0], a[1], a[0]], axis=dims[0][0])
    right = jnp.concatenate([b[0], b[0], b[1]], axis=dims[1][0])
    return dot(left, right, dims)


SQUARINGS = 11


def bounds():
    out = []
    target = 2.0**-13
    for _ in range(SQUARINGS):
        target = (2.0 * target / (1.0 + target)) ** 0.5
        out.append((1.0 + target) / (1.0 - target))
    return out


def leaf_inverse(s):
    n = s.shape[0]
    top = jnp.max(jnp.sum(jnp.abs(s), axis=0, keepdims=True), axis=1, keepdims=True)
    eye = lax.broadcasted_iota(jnp.int32, (n, n), 0) == lax.broadcasted_iota(jnp.int32, (n, n), 1)
    sp = split(s)
    biggest = jnp.max(top)
    steps = jnp.int32(0)
    for b in bounds():
        steps = steps + (biggest > b).astype(jnp.int32)

    def residual(x):
        return jnp.where(eye, 1.0, 0.0) - dot3(sp, split(x))

    def scaled(_, carry):
        x, e = carry
        e2 = e * e
        c = 2.0 / (2.0 - e2)
        x = c * (x + dot3(split(x), split(residual(x))))
        return x, e2 * 0.5 * c

    x = jnp.where(eye, 2.0 / (1.0 + top), 0.0)
    e = (top - 1.0) / (top + 1.0)
    x, _ = lax.fori_loop(0, steps + 1, scaled, (x, e))
    return x + dot3(split(x), split(residual(x)))


def invert(g, o, n):
    a = pl.ds(o, n)
    if n == LEAF:
        g[a, a] = leaf_inverse(g[a, a])
        return
    h = n // 2
    a, b = pl.ds(o, h), pl.ds(o + h, h)
    invert(g, o, h)
    low = split(g[b, a])
    y = split(dot3(low, split(g[a, a])))
    g[b, b] = g[b, b] - dot3(y, low, NT)
    invert(g, o + h, h)
    z = dot3(split(g[b, b]), y)
    g[b, a] = -z
    g[a, b] = -jnp.transpose(z)
    g[a, a] = g[a, a] + dot3(y, split(z), TN)


LEAF = 128


def sweep(g, n):
    R = 256

    def pivot(k, _):
        near = pl.ds(pl.multiple_of(k // 8 * 8, 8), 8)
        here = lax.broadcasted_iota(jnp.int32, (8, n), 0) == k % 8
        lane = lax.broadcasted_iota(jnp.int32, (8, n), 1) == k
        row = jnp.where(here, g[near, :], 0.0)
        p = jnp.sum(jnp.sum(jnp.where(lane, row, 0.0), axis=0, keepdims=True), axis=1, keepdims=True)
        w = jnp.where(lane & here, -1.0, row) / p
        for i in range(n // R):
            rows = pl.ds(i * R, R)
            column = lax.broadcasted_iota(jnp.int32, (R, n), 1) == k
            outer = lax.dot_general(
                row[:, i * R : (i + 1) * R], w, (TN, ((), ())), precision=lax.Precision.HIGHEST,
                preferred_element_type=F32,
            )
            g[rows, :] = jnp.where(column, 0.0, g[rows, :]) - outer
        g[near, :] = jnp.where(here, w, g[near, :])
        return 0

    lax.fori_loop(0, n, pivot, 0)
    for i in range(n // R):
        rows = pl.ds(i * R, R)
        g[rows, :] = -g[rows, :]


EASY = 256.0


def factor_kernel(n, a_ref, hi_ref, lo_ref, g):
    R = 256
    for i in range(n // R):
        rows = pl.ds(i * R, R)
        g[rows, : (i + 1) * R] = dot(a_ref[rows, :], a_ref[: (i + 1) * R, :], NT)
    eye = jnp.where(
        lax.broadcasted_iota(jnp.int32, (B, B), 0) == lax.broadcasted_iota(jnp.int32, (B, B), 1), 1.0, 0.0
    )
    for k in range(n // B):
        at = pl.ds(k * B, B)
        g[at, at] = g[at, at] + eye
    by_row, by_col = [], []
    for i in range(n // R):
        for j in range(i + 1):
            block = jnp.abs(g[pl.ds(i * R, R), j * R : (j + 1) * R])
            by_col.append((j, jnp.sum(block, axis=0, keepdims=True)))
            if j < i:
                by_row.append((i, block))
    most = jnp.float32(0.0)
    for i in range(n // R):
        total = sum(s for j, s in by_col if j == i)
        left = [b for j, b in by_row if j == i]
        if left:
            total = total + jnp.max(jnp.sum(sum(left), axis=1, keepdims=True), axis=0, keepdims=True)
        most = jnp.maximum(most, jnp.max(total))
    easy = most <= EASY

    @pl.when(easy)
    def _():
        invert(g, 0, n)

    @pl.when(jnp.logical_not(easy))
    def _():
        for i in range(n // R):
            for j in range(i):
                g[j * R : (j + 1) * R, i * R : (i + 1) * R] = jnp.transpose(
                    g[i * R : (i + 1) * R, j * R : (j + 1) * R]
                )
        sweep(g, n)

    for i in range(n // R):
        rows = pl.ds(i * R, R)
        hi_ref[rows, :], lo_ref[rows, :] = split(g[rows, :])


def factor(a):
    n = a.shape[0]
    return pl.pallas_call(
        functools.partial(factor_kernel, n),
        out_shape=[jax.ShapeDtypeStruct((n, n), BF16)] * 2,
        in_specs=[pl.BlockSpec(memory_space=pltpu.VMEM)],
        out_specs=[pl.BlockSpec(memory_space=pltpu.VMEM)] * 2,
        scratch_shapes=[pltpu.VMEM((n, n), F32)],
        compiler_params=pltpu.CompilerParams(vmem_limit_bytes=56 * 2**20),
    )(a)


ITERS = 2
MESH = pl.DeviceIdType.MESH
SUBC = 4
SUBF = 4
VMEM_LIMIT = 60 * 2**20


def shrink_rows(values, penalty):
    norms = jnp.sqrt(jnp.sum(values * values, axis=1, keepdims=True) + 1e-06)
    return values * (jnp.maximum(norms - penalty, 0.0) / norms)


def iterate_kernel(
    design_hbm, hi_hbm, lo_hbm, targets_hbm, weight_ref, penalty_ref, coef_hbm, coef_dual_hbm,
    tile_dual_hbm, fit_hbm, fit_dual_hbm, part_hbm, part_dual_hbm,
    coef_out, fit_out,
    design, hi, lo, coef, own_coef, own_dual, tile_dual, fit, fit_dual, targets, part, part_dual,
    coef_half, fit_half, columns,
    mine, from_core, from_z, to_x, from_x, whole, outs, from_y, to_xl, from_xl, gaps,
    load_sem, send_sem, recv_sem, store_sem,
):
    rows, cols = design.shape
    smp, feat = lax.axis_index("smp"), lax.axis_index("feat")
    xh, z, c = smp // 8, (smp // 2) % 4, smp % 2
    y, xl = feat // 2, feat % 2
    core_peer = (smp + 1 - 2 * c, feat)
    z_peer = [None] + [(xh * 8 + ((z + o) % 4) * 2 + c, feat) for o in (1, 2, 3)]
    x_peer = ((smp + 8) % 16, feat)
    y_peer = [None] + [(smp, ((y + o) % 4) * 2 + xl) for o in (1, 2, 3)]
    xl_peer = (smp, feat + 1 - 2 * xl)
    peers = [core_peer, x_peer, xl_peer] + z_peer[1:] + y_peer[1:]
    barrier = pltpu.get_barrier_semaphore()
    for peer in peers:
        pl.semaphore_signal(barrier, inc=1, device_id=peer, device_id_type=MESH)

    seg = cols // SUBC // 8
    half, part_rows = 4 * seg, 8 * seg
    fseg = rows // SUBF // 4
    fpart = 4 * fseg

    def at(u, h, q, n=1):
        return pl.ds(pl.multiple_of(u * part_rows + h * half + q * seg, seg), n * seg)

    def fat(f, q):
        return pl.ds(pl.multiple_of(f * fpart + q * fseg, fseg), fseg)

    loads = []

    def load(src, dst):
        copy = pltpu.make_async_copy(src, dst, load_sem.at[len(loads)])
        copy.start()
        loads.append(copy)
        return copy

    first = [load(coef_hbm, coef), load(tile_dual_hbm, tile_dual)]
    second = [load(part_hbm, part), load(part_dual_hbm, part_dual), load(design_hbm, design)]
    third = [load(hi_hbm, hi), load(lo_hbm, lo)]
    for u in range(SUBC):
        third.append(load(coef_dual_hbm.at[at(u, c, z)], own_dual.at[u]))
    for f in range(SUBF):
        for src, dst in ((fit_hbm, fit), (fit_dual_hbm, fit_dual), (targets_hbm, targets)):
            third.append(load(src.at[fat(f, y)], dst.at[f]))

    count = [0]
    sends = []

    def send(src, dst, peer):
        i = count[0]
        count[0] += 1
        copy = pltpu.make_async_remote_copy(
            src_ref=src, dst_ref=dst, send_sem=send_sem.at[i], recv_sem=recv_sem.at[i],
            device_id=peer, device_id_type=MESH,
        )
        copy.start()
        sends.append(copy)
        return copy

    def own_column(ref, start, n, slot):
        row = ref[pl.ds(start // B, 1), :]
        columns[slot] = jnp.transpose(jnp.broadcast_to(row, (B, B)))
        return columns[slot, pl.ds(pl.multiple_of(start % B, n), n), :][:, :1]

    def half_of_fit(f, weight):
        fit_half[f] = (fit[f] - fit_dual[f] + weight * targets[f]) / (1.0 + weight)

    for copy in first:
        copy.wait()
    for u in range(SUBC):
        own_coef[u] = coef[at(u, c, z), :]
    coef[...] = coef[...] - tile_dual[...]
    for copy in second:
        copy.wait()
    part[...] = part[...] - part_dual[...]
    M = 512
    for m in range(rows // M):
        ms = pl.ds(m * M, M)
        part[ms, :] = dot(design[ms, :], coef[...].astype(BF16)) - part[ms, :]
    for copy in third:
        copy.wait()
    weight = [own_column(weight_ref, f * fpart + y * fseg, fseg, f) for f in range(SUBF)]
    penalty = [
        own_column(penalty_ref, u * part_rows + c * half + z * seg, seg, SUBF + u) for u in range(SUBC)
    ]
    for f in range(SUBF):
        half_of_fit(f, weight[f])
    for u in range(SUBC):
        coef_half[u] = shrink_rows(own_coef[u] - own_dual[u], penalty[u])
    pl.semaphore_wait(barrier, len(peers))
    stores = []

    def store(src, dst):
        copy = pltpu.make_async_copy(src, dst, store_sem.at[len(stores)])
        copy.start()
        stores.append(copy)

    for it in range(ITERS):
        last = it == ITERS - 1
        sent = {}

        def tile_part(u):
            us = pl.ds(u * part_rows, part_rows)
            back = lax.dot_general(
                design[:, u * part_rows : (u + 1) * part_rows], sb, (((0,), (0,)), ((), ())),
                preferred_element_type=F32,
            )
            mine[it, us, :] = coef[us, :] - back
            sent["c", u] = send(mine.at[it, at(u, 1 - c, 0, 4)], from_core.at[it, u], core_peer)

        def z_reduce(u):
            sent["c", u].wait_recv()
            here = at(u, c, 0, 4)
            mine[it, here, :] = mine[it, here, :] + from_core[it, u]
            sent["z", u] = [
                send(mine.at[it, at(u, c, (z + o) % 4)], from_z.at[it, u, o - 1], z_peer[o]) for o in (2, 1, 3)
            ]

        def fit_part(f):
            fs = pl.ds(f * fpart, fpart)
            outs[it, fs, :] = dot(design[fs, :], tb)
            sent["y", f] = [
                send(outs.at[it, fat(f, (y + o) % 4)], from_y.at[it, f, o - 1], y_peer[o]) for o in (2, 1, 3)
            ]

        def x_reduce(u):
            for copy in sent["z", u]:
                copy.wait_recv()
            here = at(u, c, z)
            to_x[it, u] = (mine[it, here, :] + from_z[it, u, 0]) + (from_z[it, u, 1] + from_z[it, u, 2])
            sent["x", u] = send(to_x.at[it, u], from_x.at[it, u], x_peer)

        def xl_reduce(f):
            for copy in sent["y", f]:
                copy.wait_recv()
            here = fat(f, y)
            to_xl[it, f] = (outs[it, here, :] + from_y[it, f, 0]) + (from_y[it, f, 1] + from_y[it, f, 2])
            sent["xl", f] = send(to_xl.at[it, f], from_xl.at[it, f], xl_peer)

        def coef_step(u):
            sent["x", u].wait_recv()
            new = (coef_half[u] + (to_x[it, u] + from_x[it, u])) / 17.0
            here = at(u, c, z)
            whole[it, here, :] = new
            sent["g", u] = [send(whole.at[it, here], whole.at[it, here], z_peer[o]) for o in (2, 1, 3)]
            if not last:
                own_dual[u] = own_dual[u] + coef_half[u] - new
                own_coef[u] = new

        def fit_step(f):
            sent["xl", f].wait_recv()
            gap = (fit_half[f] - (to_xl[it, f] + from_xl[it, f])) / 9.0
            new = fit_half[f] - gap
            here = fat(f, y)
            gaps[it, here, :] = new if last else gap
            sent["w", f] = [send(gaps.at[it, here], gaps.at[it, here], y_peer[o]) for o in (2, 1, 3)]
            if not last:
                fit_dual[f] = fit_dual[f] + fit_half[f] - new
                fit[f] = new

        def to_core(u):
            for copy in sent["g", u]:
                copy.wait_recv()
            here = at(u, c, 0, 4)
            sent["d", u] = send(whole.at[it, here], whole.at[it, here], core_peer)

        def fit_end(f):
            for copy in sent["w", f]:
                copy.wait_recv()
            fs = pl.ds(f * fpart, fpart)
            if last:
                store(gaps.at[it, fs], fit_out.at[fs])
            else:
                new = outs[it, fs, :] + gaps[it, fs, :]
                part_dual[fs, :] = new - (part_dual[fs, :] - new)

        def coef_end(u):
            sent["d", u].wait_recv()
            us = pl.ds(u * part_rows, part_rows)
            if last:
                store(whole.at[it, us], coef_out.at[us])
            else:
                new = whole[it, us, :]
                local = new - (tile_dual[us, :] - new)
                coef[us, :] = local
                lb = local.astype(BF16)
                for m in range(rows // M):
                    ms = pl.ds(m * M, M)
                    prod = dot(design[ms, u * part_rows : (u + 1) * part_rows], lb)
                    part[ms, :] = prod if u == 0 else prod + part[ms, :]

        if it:
            part[...] = part[...] - part_dual[...]
        r_hi, r_lo = split(part[...])
        sb = (dot(hi[...], r_hi) + dot(lo[...], r_hi) + dot(hi[...], r_lo)).astype(BF16)
        for u in range(SUBC):
            tile_part(u)
        tb = mine[it].astype(BF16)
        if not last:
            tile_dual[...] = tile_dual[...] + mine[it]
        z_reduce(0)
        f = 0
        for u in range(1, SUBC):
            for _ in range(SUBF // SUBC):
                fit_part(f)
                f += 1
            z_reduce(u)
        while f < SUBF:
            fit_part(f)
            f += 1
        if not last:
            part_dual[...] = part_dual[...] + outs[it]
        else:
            for f in range(SUBF):
                half_of_fit(f, weight[f])
            for u in range(SUBC):
                coef_half[u] = shrink_rows(own_coef[u] - own_dual[u], penalty[u])
        order = []
        stages = [
            (0, x_reduce, SUBC), (0.5, xl_reduce, SUBF), (2, coef_step, SUBC), (2.5, fit_step, SUBF),
            (4.2, to_core, SUBC), (4.7, fit_end, SUBF), (5.2, coef_end, SUBC),
        ]
        for offset, stage, k in stages:
            for u in range(k):
                order.append((u * 4.0 / k + offset , len(order), stage, u))
        for _, _, stage, u in sorted(order, key=lambda e: e[:2]):
            stage(u)
    for copy in sends:
        copy.wait_send()
    for copy in stores:
        copy.wait()


def iterate(design, hi, lo, targets, weight, penalty, coef, coef_dual, tile_dual, fit, fit_dual, part, part_dual):
    rows, cols = design.shape
    width = coef.shape[1]
    seg = cols // SUBC // 8
    fseg = rows // SUBF // 4
    any_ = pl.BlockSpec(memory_space=pl.ANY)
    vmem = pl.BlockSpec(memory_space=pltpu.VMEM)
    f32 = lambda *shape: pltpu.VMEM(shape + (width,), F32)
    n_copies = ITERS * (9 * SUBC + 7 * SUBF)
    return pl.pallas_call(
        iterate_kernel,
        out_shape=[jax.ShapeDtypeStruct((cols, width), F32), jax.ShapeDtypeStruct((rows, width), F32)],
        in_specs=[any_] * 4 + [vmem] * 2 + [any_] * 7,
        out_specs=[any_] * 2,
        scratch_shapes=[
            pltpu.VMEM((rows, cols), BF16), pltpu.VMEM((rows, rows), BF16), pltpu.VMEM((rows, rows), BF16),
            f32(cols), f32(SUBC, seg), f32(SUBC, seg), f32(cols), f32(SUBF, fseg), f32(SUBF, fseg), f32(SUBF, fseg),
            f32(rows), f32(rows), f32(SUBC, seg), f32(SUBF, fseg), pltpu.VMEM((SUBC + SUBF, B, B), F32),
            f32(ITERS, cols), f32(ITERS, SUBC, 4 * seg), f32(ITERS, SUBC, 3, seg),
            f32(ITERS, SUBC, seg), f32(ITERS, SUBC, seg), f32(ITERS, cols),
            f32(ITERS, rows), f32(ITERS, SUBF, 3, fseg), f32(ITERS, SUBF, fseg),
            f32(ITERS, SUBF, fseg), f32(ITERS, rows),
            pltpu.SemaphoreType.DMA((7 + SUBC + 3 * SUBF,)), pltpu.SemaphoreType.DMA((n_copies,)),
            pltpu.SemaphoreType.DMA((n_copies,)), pltpu.SemaphoreType.DMA((SUBC + SUBF,)),
        ],
        compiler_params=pltpu.CompilerParams(
            collective_id=0, has_side_effects=True, vmem_limit_bytes=VMEM_LIMIT
        ),
    )(design, hi, lo, targets, weight.reshape(-1, B), penalty.reshape(-1, B), coef, coef_dual, tile_dual, fit,
      fit_dual, part, part_dual)


def per_device(design, targets, weight, penalty, coef, coef_dual, tile_dual, fit, fit_dual, part, part_dual):
    hi, lo = factor(design)
    return tuple(iterate(design, hi, lo, targets, weight, penalty, coef, coef_dual, tile_dual[0], fit, fit_dual,
                   part[0], part_dual[0]))


def solution(mesh):
    return jax.shard_map(
        per_device,
        mesh=mesh,
        in_specs=(
            P("smp", "feat"),
            P("smp", None),
            P("smp"),
            P("feat"),
            P("feat", None),
            P("feat", None),
            P("smp", "feat", None),
            P("smp", None),
            P("smp", None),
            P("feat", "smp", None),
            P("feat", "smp", None),
        ),
        out_specs=(P("feat", None), P("smp", None)),
        check_vma=False,
    )
```

```python
import functools
import jax
import jax.numpy as jnp
from jax import lax
from jax.experimental import pallas as pl
from jax.experimental.pallas import tpu as pltpu
from jax.sharding import PartitionSpec as P

F32, BF16 = jnp.float32, jnp.bfloat16
B = 128
NN, NT, TN = ((1,), (0,)), ((1,), (1,)), ((0,), (0,))


def split(x):
    hi = x.astype(BF16)
    return hi, (x - hi.astype(F32)).astype(BF16)


def dot(a, b, dims=NN):
    return lax.dot_general(a, b, (dims, ((), ())), preferred_element_type=F32)


def dot3(a, b, dims=NN):
    left = jnp.concatenate([a[0], a[1], a[0]], axis=dims[0][0])
    right = jnp.concatenate([b[0], b[0], b[1]], axis=dims[1][0])
    return dot(left, right, dims)


SQUARINGS = 11


def bounds():
    out = []
    target = 2.0**-13
    for _ in range(SQUARINGS):
        target = (2.0 * target / (1.0 + target)) ** 0.5
        out.append((1.0 + target) / (1.0 - target))
    return out


def leaf_inverse(s):
    n = s.shape[0]
    top = jnp.max(jnp.sum(jnp.abs(s), axis=0, keepdims=True), axis=1, keepdims=True)
    eye = lax.broadcasted_iota(jnp.int32, (n, n), 0) == lax.broadcasted_iota(jnp.int32, (n, n), 1)
    biggest = jnp.max(top)
    steps = jnp.int32(0)
    for b in bounds():
        steps = steps + (biggest > b).astype(jnp.int32)

    def scaled(_, carry):
        both, e = carry
        e2 = e * e
        c = 2.0 / (2.0 - e2)
        pair = split(both)
        prod = dot3(pair, (pair[0][n:], pair[1][n:]))
        x = c * (both[:n] + prod[:n])
        r = jnp.where(eye, 1.0 - c, 0.0) + c * prod[n:]
        return jnp.concatenate([x, r], axis=0), e2 * 0.5 * c

    start = 2.0 / (1.0 + top)
    both = jnp.concatenate([jnp.where(eye, start, 0.0), jnp.where(eye, 1.0, 0.0) - start * s], axis=0)
    both, _ = lax.fori_loop(0, steps + 1, scaled, (both, (top - 1.0) / (top + 1.0)))
    x = both[:n]
    pair = split(x)
    residual = jnp.where(eye, 1.0, 0.0) - dot3(split(s), pair)
    return x + dot(pair[0], residual.astype(BF16))


def invert(g, o, n):
    a = pl.ds(o, n)
    if n == LEAF:
        g[a, a] = leaf_inverse(g[a, a])
        return
    h = n // 2
    a, b = pl.ds(o, h), pl.ds(o + h, h)
    invert(g, o, h)
    low = split(g[b, a])
    y = split(dot3(low, split(g[a, a])))
    g[b, b] = g[b, b] - dot3(y, low, NT)
    invert(g, o + h, h)
    z = dot3(split(g[b, b]), y)
    g[b, a] = -z
    g[a, b] = -jnp.transpose(z)
    g[a, a] = g[a, a] + dot3(y, split(z), TN)


LEAF = 256


def sweep(g, n):
    R = 256

    def pivot(k, _):
        near = pl.ds(pl.multiple_of(k // 8 * 8, 8), 8)
        here = lax.broadcasted_iota(jnp.int32, (8, n), 0) == k % 8
        lane = lax.broadcasted_iota(jnp.int32, (8, n), 1) == k
        row = jnp.where(here, g[near, :], 0.0)
        p = jnp.sum(jnp.sum(jnp.where(lane, row, 0.0), axis=0, keepdims=True), axis=1, keepdims=True)
        w = jnp.where(lane & here, -1.0, row) / p
        for i in range(n // R):
            rows = pl.ds(i * R, R)
            column = lax.broadcasted_iota(jnp.int32, (R, n), 1) == k
            outer = lax.dot_general(
                row[:, i * R : (i + 1) * R], w, (TN, ((), ())), precision=lax.Precision.HIGHEST,
                preferred_element_type=F32,
            )
            g[rows, :] = jnp.where(column, 0.0, g[rows, :]) - outer
        g[near, :] = jnp.where(here, w, g[near, :])
        return 0

    lax.fori_loop(0, n, pivot, 0)
    for i in range(n // R):
        rows = pl.ds(i * R, R)
        g[rows, :] = -g[rows, :]


EASY = 256.0


def factor_kernel(
    design_hbm, coef_hbm, dual_hbm, part_hbm, part_dual_hbm,
    hi_out, lo_out, local_out, target_out, resid_out,
    a_ref, coef, dual, part, part_dual, resid, hi_ref, lo_ref, g, in_sem, out_sem,
):
    n = a_ref.shape[0]
    R = 256
    loads, stores = [], []

    def load(src, dst):
        loads.append(pltpu.make_async_copy(src, dst, in_sem.at[len(loads)]))
        loads[-1].start()

    def store(src, dst):
        stores.append(pltpu.make_async_copy(src, dst, out_sem.at[len(stores)]))
        stores[-1].start()

    for i in range(n // R):
        load(design_hbm.at[pl.ds(i * R, R)], a_ref.at[pl.ds(i * R, R)])
    for src, dst in ((coef_hbm, coef), (dual_hbm, dual), (part_hbm, part), (part_dual_hbm, part_dual)):
        load(src, dst)
    for i in range(n // R):
        rows = pl.ds(i * R, R)
        loads[i].wait()
        g[rows, : (i + 1) * R] = dot(a_ref[rows, :], a_ref[: (i + 1) * R, :], NT)
    eye = jnp.where(
        lax.broadcasted_iota(jnp.int32, (B, B), 0) == lax.broadcasted_iota(jnp.int32, (B, B), 1), 1.0, 0.0
    )
    for k in range(n // B):
        at = pl.ds(k * B, B)
        g[at, at] = g[at, at] + eye
    for copy in loads[n // R :]:
        copy.wait()
    coef[...] = coef[...] - dual[...]
    store(coef, local_out)
    part[...] = part[...] - part_dual[...]
    store(part, target_out)
    cb = coef[...].astype(BF16)
    for i in range(n // 512):
        rows = pl.ds(i * 512, 512)
        resid[rows, :] = dot(a_ref[rows, :], cb) - part[rows, :]
    store(resid, resid_out)
    by_row, by_col = [], []
    for i in range(n // R):
        for j in range(i + 1):
            block = jnp.abs(g[pl.ds(i * R, R), j * R : (j + 1) * R])
            by_col.append((j, jnp.sum(block, axis=0, keepdims=True)))
            if j < i:
                by_row.append((i, block))
    most = jnp.float32(0.0)
    for i in range(n // R):
        total = sum(s for j, s in by_col if j == i)
        left = [b for j, b in by_row if j == i]
        if left:
            total = total + jnp.max(jnp.sum(sum(left), axis=1, keepdims=True), axis=0, keepdims=True)
        most = jnp.maximum(most, jnp.max(total))
    easy = most <= EASY

    @pl.when(easy)
    def _():
        invert(g, 0, n)

    @pl.when(jnp.logical_not(easy))
    def _():
        for i in range(n // R):
            for j in range(i):
                g[j * R : (j + 1) * R, i * R : (i + 1) * R] = jnp.transpose(
                    g[i * R : (i + 1) * R, j * R : (j + 1) * R]
                )
        sweep(g, n)

    for i in range(n // R):
        rows = pl.ds(i * R, R)
        hi_ref[rows, :], lo_ref[rows, :] = split(g[rows, :])
        store(hi_ref.at[rows], hi_out.at[rows])
        store(lo_ref.at[rows], lo_out.at[rows])
    for copy in stores:
        copy.wait()


def factor(design, coef, dual, part, part_dual):
    n, cols = design.shape
    width = coef.shape[1]
    any_ = pl.BlockSpec(memory_space=pl.ANY)
    square = jax.ShapeDtypeStruct((n, n), BF16)
    tall = jax.ShapeDtypeStruct((cols, width), F32)
    flat = jax.ShapeDtypeStruct((n, width), F32)
    vmem = lambda s: pltpu.VMEM(s.shape, s.dtype)
    return pl.pallas_call(
        factor_kernel,
        out_shape=[square, square, tall, flat, flat],
        in_specs=[any_] * 5,
        out_specs=[any_] * 5,
        scratch_shapes=[
            vmem(design), vmem(tall), vmem(tall), vmem(flat), vmem(flat), vmem(flat), vmem(square), vmem(square),
            pltpu.VMEM((n, n), F32), pltpu.SemaphoreType.DMA((4 + n // 256,)), pltpu.SemaphoreType.DMA((3 + n // 128,)),
        ],
        compiler_params=pltpu.CompilerParams(vmem_limit_bytes=56 * 2**20),
    )(design, coef, dual, part, part_dual)


ITERS = 2
MESH = pl.DeviceIdType.MESH
SUBC = 4
SUBF = 4
VMEM_LIMIT = 60 * 2**20


def shrink_rows(values, penalty):
    norms = jnp.sqrt(jnp.sum(values * values, axis=1, keepdims=True) + 1e-06)
    return values * (jnp.maximum(norms - penalty, 0.0) / norms)


def iterate_kernel(
    design_hbm, hi_hbm, lo_hbm, local_hbm, target_hbm, resid_hbm, targets_hbm, weight_ref, penalty_ref,
    coef_hbm, coef_dual_hbm, tile_dual_hbm, fit_hbm, fit_dual_hbm, part_dual_hbm,
    coef_out, fit_out,
    design, hi, lo, local, own_coef, own_dual, tile_dual, fit, fit_dual, targets, target, resid, part_dual,
    coef_half, fit_half, columns, tiles,
    mine, from_core, from_z, to_x, from_x, whole, outs, from_y, to_xl, from_xl, gaps,
    load_sem, send_sem, recv_sem, store_sem,
):
    rows, cols = design.shape
    smp, feat = lax.axis_index("smp"), lax.axis_index("feat")
    xh, z, c = smp // 8, (smp // 2) % 4, smp % 2
    y, xl = feat // 2, feat % 2
    core_peer = (smp + 1 - 2 * c, feat)
    z_peer = [None] + [(xh * 8 + ((z + o) % 4) * 2 + c, feat) for o in (1, 2, 3)]
    x_peer = ((smp + 8) % 16, feat)
    y_peer = [None] + [(smp, ((y + o) % 4) * 2 + xl) for o in (1, 2, 3)]
    xl_peer = (smp, feat + 1 - 2 * xl)
    peers = [core_peer, x_peer, xl_peer] + z_peer[1:] + y_peer[1:]
    barrier = pltpu.get_barrier_semaphore()
    for peer in peers:
        pl.semaphore_signal(barrier, inc=1, device_id=peer, device_id_type=MESH)

    seg = cols // SUBC // 8
    half, part_rows = 4 * seg, 8 * seg
    fseg = rows // SUBF // 4
    fpart = 4 * fseg

    def at(u, h, q, n=1):
        return pl.ds(pl.multiple_of(u * part_rows + h * half + q * seg, seg), n * seg)

    def fat(f, q):
        return pl.ds(pl.multiple_of(f * fpart + q * fseg, fseg), fseg)

    loads = []

    def load(src, dst):
        copy = pltpu.make_async_copy(src, dst, load_sem.at[len(loads)])
        copy.start()
        loads.append(copy)
        return copy

    first = [load(hi_hbm, hi), load(resid_hbm, resid), load(lo_hbm, lo), load(target_hbm, target)]
    second = [load(design_hbm, design), load(local_hbm, local)]
    third = []
    for f in range(SUBF):
        for src, dst in ((fit_hbm, fit), (fit_dual_hbm, fit_dual), (targets_hbm, targets)):
            third.append(load(src.at[fat(f, y)], dst.at[f]))
    for u in range(SUBC):
        third.append(load(coef_hbm.at[at(u, c, z)], own_coef.at[u]))
        third.append(load(coef_dual_hbm.at[at(u, c, z)], own_dual.at[u]))
    third += [load(tile_dual_hbm, tile_dual), load(part_dual_hbm, part_dual)]

    count = [0]
    sends = []

    def send(src, dst, peer):
        i = count[0]
        count[0] += 1
        copy = pltpu.make_async_remote_copy(
            src_ref=src, dst_ref=dst, send_sem=send_sem.at[i], recv_sem=recv_sem.at[i],
            device_id=peer, device_id_type=MESH,
        )
        copy.start()
        sends.append(copy)
        return copy

    def own_column(ref, start, n, slot):
        row = ref[pl.ds(start // B, 1), :]
        columns[slot] = jnp.transpose(jnp.broadcast_to(row, (B, B)))
        return columns[slot, pl.ds(pl.multiple_of(start % B, n), n), :][:, :1]

    def half_of_fit(f, weight):
        fit_half[f] = (fit[f] - fit_dual[f] + weight * targets[f]) / (1.0 + weight)

    weight = [own_column(weight_ref, f * fpart + y * fseg, fseg, f) for f in range(SUBF)]
    penalty = [
        own_column(penalty_ref, u * part_rows + c * half + z * seg, seg, SUBF + u) for u in range(SUBC)
    ]
    M = 512
    stores = []

    def store(src, dst):
        copy = pltpu.make_async_copy(src, dst, store_sem.at[len(stores)])
        copy.start()
        stores.append(copy)

    for it in range(ITERS):
        last = it == ITERS - 1
        sent = {}

        def tile_part(u):
            us = pl.ds(u * part_rows, part_rows)
            back = lax.dot_general(
                design[:, u * part_rows : (u + 1) * part_rows], sb, (((0,), (0,)), ((), ())),
                preferred_element_type=F32,
            )
            tile = local[us, :] - back
            mine[it, us, :] = tile
            if not last:
                tiles[us, :] = tile
            sent["c", u] = send(mine.at[it, at(u, 1 - c, 0, 4)], from_core.at[it, u], core_peer)

        def z_reduce(u):
            sent["c", u].wait_recv()
            here = at(u, c, 0, 4)
            mine[it, here, :] = mine[it, here, :] + from_core[it, u]
            sent["z", u] = [
                send(mine.at[it, at(u, c, (z + o) % 4)], from_z.at[it, u, o - 1], z_peer[o]) for o in (2, 1, 3)
            ]

        def fit_part(f):
            sent["y", f] = [
                send(outs.at[it, fat(f, (y + o) % 4)], from_y.at[it, f, o - 1], y_peer[o]) for o in (2, 1, 3)
            ]

        def x_reduce(u):
            for copy in sent["z", u]:
                copy.wait_recv()
            here = at(u, c, z)
            to_x[it, u] = (mine[it, here, :] + from_z[it, u, 0]) + (from_z[it, u, 1] + from_z[it, u, 2])
            sent["x", u] = send(to_x.at[it, u], from_x.at[it, u], x_peer)

        def xl_reduce(f):
            for copy in sent["y", f]:
                copy.wait_recv()
            here = fat(f, y)
            to_xl[it, f] = (outs[it, here, :] + from_y[it, f, 0]) + (from_y[it, f, 1] + from_y[it, f, 2])
            sent["xl", f] = send(to_xl.at[it, f], from_xl.at[it, f], xl_peer)

        def coef_step(u):
            sent["x", u].wait_recv()
            new = (coef_half[u] + (to_x[it, u] + from_x[it, u])) / 17.0
            here = at(u, c, z)
            whole[it, here, :] = new
            sent["g", u] = [send(whole.at[it, here], whole.at[it, here], z_peer[o]) for o in (2, 1, 3)]
            if not last:
                own_dual[u] = own_dual[u] + coef_half[u] - new
                own_coef[u] = new

        def fit_step(f):
            sent["xl", f].wait_recv()
            gap = (fit_half[f] - (to_xl[it, f] + from_xl[it, f])) / 9.0
            new = fit_half[f] - gap
            here = fat(f, y)
            gaps[it, here, :] = new if last else gap
            sent["w", f] = [send(gaps.at[it, here], gaps.at[it, here], y_peer[o]) for o in (2, 1, 3)]
            if not last:
                fit_dual[f] = fit_dual[f] + fit_half[f] - new
                fit[f] = new

        def to_core(u):
            for copy in sent["g", u]:
                copy.wait_recv()
            here = at(u, c, 0, 4)
            sent["d", u] = send(whole.at[it, here], whole.at[it, here], core_peer)

        def fit_end(f):
            for copy in sent["w", f]:
                copy.wait_recv()
            fs = pl.ds(f * fpart, fpart)
            if last:
                store(gaps.at[it, fs], fit_out.at[fs])
            else:
                new = outs[it, fs, :] + gaps[it, fs, :]
                target[fs, :] = new - (part_dual[fs, :] - new)

        def coef_end(u):
            sent["d", u].wait_recv()
            us = pl.ds(u * part_rows, part_rows)
            if last:
                store(whole.at[it, us], coef_out.at[us])
            else:
                new = whole[it, us, :]
                here = new - (tile_dual[us, :] - new)
                local[us, :] = here
                lb = here.astype(BF16)
                for m in range(rows // M):
                    ms = pl.ds(m * M, M)
                    prod = dot(design[ms, u * part_rows : (u + 1) * part_rows], lb)
                    resid[ms, :] = prod if u == 0 else prod + resid[ms, :]

        if it == 0:
            for copy in first:
                copy.wait()
        else:
            resid[...] = resid[...] - target[...]
        r_hi, r_lo = split(resid[...])
        solved = []
        f = 0
        for m in range(rows // M):
            ms = pl.ds(m * M, M)
            s = dot(hi[ms, :], r_hi) + dot(lo[ms, :], r_hi) + dot(hi[ms, :], r_lo)
            solved.append(s.astype(BF16))
            outs[it, ms, :] = target[ms, :] + s
            if it == 0 and m == 0:
                pl.semaphore_wait(barrier, len(peers))
            while (f + 1) * fpart <= (m + 1) * M:
                fit_part(f)
                f += 1
        sb = jnp.concatenate(solved, axis=0)
        if it == 0:
            for copy in second:
                copy.wait()
        for u in range(SUBC):
            tile_part(u)
            if u:
                z_reduce(u - 1)
        z_reduce(SUBC - 1)
        if it == 0:
            for copy in third:
                copy.wait()
        for f in range(SUBF):
            half_of_fit(f, weight[f])
        for u in range(SUBC):
            coef_half[u] = shrink_rows(own_coef[u] - own_dual[u], penalty[u])
        if not last:
            part_dual[...] = part_dual[...] + outs[it]
            for u in range(SUBC):
                us = pl.ds(u * part_rows, part_rows)
                tile_dual[us, :] = tile_dual[us, :] + tiles[us, :]
        order = []
        stages = [
            (0, x_reduce, SUBC), (0.5, xl_reduce, SUBF), (2, coef_step, SUBC), (2.5, fit_step, SUBF),
            (4.2, to_core, SUBC), (4.7, fit_end, SUBF), (5.2, coef_end, SUBC),
        ]
        for offset, stage, k in stages:
            for u in range(k):
                order.append((u * 4.0 / k + offset , len(order), stage, u))
        for _, _, stage, u in sorted(order, key=lambda e: e[:2]):
            stage(u)
    for copy in sends:
        copy.wait_send()
    for copy in stores:
        copy.wait()


def iterate(
    design, hi, lo, local, target, resid, targets, weight, penalty, coef, coef_dual, tile_dual, fit, fit_dual, part_dual
):
    rows, cols = design.shape
    width = coef.shape[1]
    seg = cols // SUBC // 8
    fseg = rows // SUBF // 4
    any_ = pl.BlockSpec(memory_space=pl.ANY)
    vmem = pl.BlockSpec(memory_space=pltpu.VMEM)
    f32 = lambda *shape: pltpu.VMEM(shape + (width,), F32)
    n_copies = ITERS * (9 * SUBC + 7 * SUBF)
    return pl.pallas_call(
        iterate_kernel,
        out_shape=[jax.ShapeDtypeStruct((cols, width), F32), jax.ShapeDtypeStruct((rows, width), F32)],
        in_specs=[any_] * 7 + [vmem] * 2 + [any_] * 6,
        out_specs=[any_] * 2,
        scratch_shapes=[
            pltpu.VMEM((rows, cols), BF16), pltpu.VMEM((rows, rows), BF16), pltpu.VMEM((rows, rows), BF16),
            f32(cols), f32(SUBC, seg), f32(SUBC, seg), f32(cols), f32(SUBF, fseg), f32(SUBF, fseg), f32(SUBF, fseg),
            f32(rows), f32(rows), f32(rows), f32(SUBC, seg), f32(SUBF, fseg), pltpu.VMEM((SUBC + SUBF, B, B), F32), f32(cols),
            f32(ITERS, cols), f32(ITERS, SUBC, 4 * seg), f32(ITERS, SUBC, 3, seg),
            f32(ITERS, SUBC, seg), f32(ITERS, SUBC, seg), f32(ITERS, cols),
            f32(ITERS, rows), f32(ITERS, SUBF, 3, fseg), f32(ITERS, SUBF, fseg),
            f32(ITERS, SUBF, fseg), f32(ITERS, rows),
            pltpu.SemaphoreType.DMA((8 + 2 * SUBC + 3 * SUBF,)), pltpu.SemaphoreType.DMA((n_copies,)),
            pltpu.SemaphoreType.DMA((n_copies,)), pltpu.SemaphoreType.DMA((SUBC + SUBF,)),
        ],
        compiler_params=pltpu.CompilerParams(
            collective_id=0, has_side_effects=True, vmem_limit_bytes=VMEM_LIMIT
        ),
    )(design, hi, lo, local, target, resid, targets, weight.reshape(-1, B), penalty.reshape(-1, B), coef, coef_dual,
      tile_dual, fit, fit_dual, part_dual)


def per_device(design, targets, weight, penalty, coef, coef_dual, tile_dual, fit, fit_dual, part, part_dual):
    tile_dual, part, part_dual = tile_dual[0], part[0], part_dual[0]
    hi, lo, local, target, resid = factor(design, coef, tile_dual, part, part_dual)
    return tuple(
        iterate(
            design, hi, lo, local, target, resid, targets, weight, penalty, coef, coef_dual, tile_dual, fit, fit_dual,
            part_dual,
        )
    )


def solution(mesh):
    return jax.shard_map(
        per_device,
        mesh=mesh,
        in_specs=(
            P("smp", "feat"),
            P("smp", None),
            P("smp"),
            P("feat"),
            P("feat", None),
            P("feat", None),
            P("smp", "feat", None),
            P("smp", None),
            P("smp", None),
            P("feat", "smp", None),
            P("feat", "smp", None),
        ),
        out_specs=(P("feat", None), P("smp", None)),
        check_vma=False,
    )
```

```python
import functools
import jax
import jax.numpy as jnp
from jax import lax
from jax.experimental import pallas as pl
from jax.experimental.pallas import tpu as pltpu
from jax.sharding import PartitionSpec as P

F32, BF16 = jnp.float32, jnp.bfloat16
B = 128
NN, NT, TN = ((1,), (0,)), ((1,), (1,)), ((0,), (0,))


def split(x):
    hi = x.astype(BF16)
    return hi, (x - hi.astype(F32)).astype(BF16)


def dot(a, b, dims=NN):
    return lax.dot_general(a, b, (dims, ((), ())), preferred_element_type=F32)


def dot3(a, b, dims=NN):
    left = jnp.concatenate([a[0], a[1], a[0]], axis=dims[0][0])
    right = jnp.concatenate([b[0], b[0], b[1]], axis=dims[1][0])
    return dot(left, right, dims)


SQUARINGS = 11


def bounds():
    out = []
    target = 2.0**-13
    for _ in range(SQUARINGS):
        target = (2.0 * target / (1.0 + target)) ** 0.5
        out.append((1.0 + target) / (1.0 - target))
    return out


def leaf_inverse(s):
    n = s.shape[0]
    top = jnp.max(jnp.sum(jnp.abs(s), axis=0, keepdims=True), axis=1, keepdims=True)
    eye = lax.broadcasted_iota(jnp.int32, (n, n), 0) == lax.broadcasted_iota(jnp.int32, (n, n), 1)
    biggest = jnp.max(top)
    steps = jnp.int32(0)
    for b in bounds():
        steps = steps + (biggest > b).astype(jnp.int32)

    def scaled(_, carry):
        both, e = carry
        e2 = e * e
        c = 2.0 / (2.0 - e2)
        pair = split(both)
        prod = dot3(pair, (pair[0][n:], pair[1][n:]))
        x = c * (both[:n] + prod[:n])
        r = jnp.where(eye, 1.0 - c, 0.0) + c * prod[n:]
        return jnp.concatenate([x, r], axis=0), e2 * 0.5 * c

    start = 2.0 / (1.0 + top)
    both = jnp.concatenate([jnp.where(eye, start, 0.0), jnp.where(eye, 1.0, 0.0) - start * s], axis=0)
    both, _ = lax.fori_loop(0, steps + 1, scaled, (both, (top - 1.0) / (top + 1.0)))
    x = both[:n]
    pair = split(x)
    residual = jnp.where(eye, 1.0, 0.0) - dot3(split(s), pair)
    return x + dot(pair[0], residual.astype(BF16))


def invert(g, o, n):
    a = pl.ds(o, n)
    if n == LEAF:
        g[a, a] = leaf_inverse(g[a, a])
        return
    h = n // 2
    a, b = pl.ds(o, h), pl.ds(o + h, h)
    invert(g, o, h)
    low = split(g[b, a])
    y = split(dot3(low, split(g[a, a])))
    g[b, b] = g[b, b] - dot3(y, low, NT)
    invert(g, o + h, h)
    z = dot3(split(g[b, b]), y)
    g[b, a] = -z
    g[a, b] = -jnp.transpose(z)
    g[a, a] = g[a, a] + dot3(y, split(z), TN)


LEAF = 256


def sweep(g, n):
    R = 256

    def pivot(k, _):
        near = pl.ds(pl.multiple_of(k // 8 * 8, 8), 8)
        here = lax.broadcasted_iota(jnp.int32, (8, n), 0) == k % 8
        lane = lax.broadcasted_iota(jnp.int32, (8, n), 1) == k
        row = jnp.where(here, g[near, :], 0.0)
        p = jnp.sum(jnp.sum(jnp.where(lane, row, 0.0), axis=0, keepdims=True), axis=1, keepdims=True)
        w = jnp.where(lane & here, -1.0, row) / p
        for i in range(n // R):
            rows = pl.ds(i * R, R)
            column = lax.broadcasted_iota(jnp.int32, (R, n), 1) == k
            outer = lax.dot_general(
                row[:, i * R : (i + 1) * R], w, (TN, ((), ())), precision=lax.Precision.HIGHEST,
                preferred_element_type=F32,
            )
            g[rows, :] = jnp.where(column, 0.0, g[rows, :]) - outer
        g[near, :] = jnp.where(here, w, g[near, :])
        return 0

    lax.fori_loop(0, n, pivot, 0)
    for i in range(n // R):
        rows = pl.ds(i * R, R)
        g[rows, :] = -g[rows, :]


EASY = 256.0


def factor_kernel(
    design_hbm, coef_hbm, dual_hbm, part_hbm, part_dual_hbm,
    hi_out, lo_out, local_out, target_out, resid_out,
    a_ref, coef, dual, part, part_dual, resid, hi_ref, lo_ref, g, in_sem, out_sem,
):
    n = a_ref.shape[0]
    R = 256
    loads, stores = [], []

    def load(src, dst):
        loads.append(pltpu.make_async_copy(src, dst, in_sem.at[len(loads)]))
        loads[-1].start()

    def store(src, dst):
        stores.append(pltpu.make_async_copy(src, dst, out_sem.at[len(stores)]))
        stores[-1].start()

    for i in range(n // R):
        load(design_hbm.at[pl.ds(i * R, R)], a_ref.at[pl.ds(i * R, R)])
    for src, dst in ((coef_hbm, coef), (dual_hbm, dual), (part_hbm, part), (part_dual_hbm, part_dual)):
        load(src, dst)
    for i in range(n // R):
        rows = pl.ds(i * R, R)
        loads[i].wait()
        g[rows, : (i + 1) * R] = dot(a_ref[rows, :], a_ref[: (i + 1) * R, :], NT)
    eye = jnp.where(
        lax.broadcasted_iota(jnp.int32, (B, B), 0) == lax.broadcasted_iota(jnp.int32, (B, B), 1), 1.0, 0.0
    )
    for k in range(n // B):
        at = pl.ds(k * B, B)
        g[at, at] = g[at, at] + eye
    for copy in loads[n // R :]:
        copy.wait()
    coef[...] = coef[...] - dual[...]
    store(coef, local_out)
    part[...] = part[...] - part_dual[...]
    store(part, target_out)
    cb = coef[...].astype(BF16)
    for i in range(n // 512):
        rows = pl.ds(i * 512, 512)
        resid[rows, :] = dot(a_ref[rows, :], cb) - part[rows, :]
    store(resid, resid_out)
    by_row, by_col = [], []
    for i in range(n // R):
        for j in range(i + 1):
            block = jnp.abs(g[pl.ds(i * R, R), j * R : (j + 1) * R])
            by_col.append((j, jnp.sum(block, axis=0, keepdims=True)))
            if j < i:
                by_row.append((i, block))
    most = jnp.float32(0.0)
    for i in range(n // R):
        total = sum(s for j, s in by_col if j == i)
        left = [b for j, b in by_row if j == i]
        if left:
            total = total + jnp.max(jnp.sum(sum(left), axis=1, keepdims=True), axis=0, keepdims=True)
        most = jnp.maximum(most, jnp.max(total))
    easy = most <= EASY

    @pl.when(easy)
    def _():
        invert(g, 0, n)

    @pl.when(jnp.logical_not(easy))
    def _():
        for i in range(n // R):
            for j in range(i):
                g[j * R : (j + 1) * R, i * R : (i + 1) * R] = jnp.transpose(
                    g[i * R : (i + 1) * R, j * R : (j + 1) * R]
                )
        sweep(g, n)

    for i in range(n // R):
        rows = pl.ds(i * R, R)
        hi_ref[rows, :], lo_ref[rows, :] = split(g[rows, :])
        store(hi_ref.at[rows], hi_out.at[rows])
        store(lo_ref.at[rows], lo_out.at[rows])
    for copy in stores:
        copy.wait()


def factor(design, coef, dual, part, part_dual):
    n, cols = design.shape
    width = coef.shape[1]
    any_ = pl.BlockSpec(memory_space=pl.ANY)
    square = jax.ShapeDtypeStruct((n, n), BF16)
    tall = jax.ShapeDtypeStruct((cols, width), F32)
    flat = jax.ShapeDtypeStruct((n, width), F32)
    vmem = lambda s: pltpu.VMEM(s.shape, s.dtype)
    return pl.pallas_call(
        factor_kernel,
        out_shape=[square, square, tall, flat, flat],
        in_specs=[any_] * 5,
        out_specs=[any_] * 5,
        scratch_shapes=[
            vmem(design), vmem(tall), vmem(tall), vmem(flat), vmem(flat), vmem(flat), vmem(square), vmem(square),
            pltpu.VMEM((n, n), F32), pltpu.SemaphoreType.DMA((4 + n // 256,)), pltpu.SemaphoreType.DMA((3 + n // 128,)),
        ],
        compiler_params=pltpu.CompilerParams(vmem_limit_bytes=56 * 2**20),
    )(design, coef, dual, part, part_dual)


ITERS = 2
MESH = pl.DeviceIdType.MESH
SUBC = 4
SUBF = 4
VMEM_LIMIT = 60 * 2**20


def shrink_rows(values, penalty):
    norms = jnp.sqrt(jnp.sum(values * values, axis=1, keepdims=True) + 1e-06)
    return values * (jnp.maximum(norms - penalty, 0.0) / norms)


def iterate_kernel(
    design_hbm, hi_hbm, lo_hbm, local_hbm, target_hbm, resid_hbm, targets_hbm, weight_ref, penalty_ref,
    coef_hbm, coef_dual_hbm, tile_dual_hbm, fit_hbm, fit_dual_hbm, part_dual_hbm,
    coef_out, fit_out,
    design, hi, lo, local, own_coef, own_dual, tile_dual, fit, fit_dual, targets, target, resid, part_dual,
    coef_half, fit_half, columns, tiles,
    mine, from_core, from_z, to_x, from_x, whole, outs, from_y, to_xl, from_xl, gaps,
    load_sem, send_sem, recv_sem, store_sem,
):
    rows, cols = design.shape
    smp, feat = lax.axis_index("smp"), lax.axis_index("feat")
    xh, z, c = smp // 8, (smp // 2) % 4, smp % 2
    y, xl = feat // 2, feat % 2
    core_peer = (smp + 1 - 2 * c, feat)
    z_peer = [None] + [(xh * 8 + ((z + o) % 4) * 2 + c, feat) for o in (1, 2, 3)]
    x_peer = ((smp + 8) % 16, feat)
    y_peer = [None] + [(smp, ((y + o) % 4) * 2 + xl) for o in (1, 2, 3)]
    xl_peer = (smp, feat + 1 - 2 * xl)
    peers = [core_peer, x_peer, xl_peer] + z_peer[1:] + y_peer[1:]
    barrier = pltpu.get_barrier_semaphore()
    for peer in peers:
        pl.semaphore_signal(barrier, inc=1, device_id=peer, device_id_type=MESH)

    seg = cols // SUBC // 8
    half, part_rows = 4 * seg, 8 * seg
    fseg = rows // SUBF // 4
    fpart = 4 * fseg

    def at(u, h, q, n=1):
        return pl.ds(pl.multiple_of(u * part_rows + h * half + q * seg, seg), n * seg)

    def fat(f, q):
        return pl.ds(pl.multiple_of(f * fpart + q * fseg, fseg), fseg)

    loads = []

    def load(src, dst):
        copy = pltpu.make_async_copy(src, dst, load_sem.at[len(loads)])
        copy.start()
        loads.append(copy)
        return copy

    first = [load(hi_hbm, hi), load(resid_hbm, resid), load(lo_hbm, lo), load(target_hbm, target)]
    second = [load(design_hbm, design), load(local_hbm, local)]
    third = []
    for f in range(SUBF):
        for src, dst in ((fit_hbm, fit), (fit_dual_hbm, fit_dual), (targets_hbm, targets)):
            third.append(load(src.at[fat(f, y)], dst.at[f]))
    for u in range(SUBC):
        third.append(load(coef_hbm.at[at(u, c, z)], own_coef.at[u]))
        third.append(load(coef_dual_hbm.at[at(u, c, z)], own_dual.at[u]))
    third += [load(tile_dual_hbm, tile_dual), load(part_dual_hbm, part_dual)]

    count = [0]
    sends = []

    def send(src, dst, peer):
        i = count[0]
        count[0] += 1
        copy = pltpu.make_async_remote_copy(
            src_ref=src, dst_ref=dst, send_sem=send_sem.at[i], recv_sem=recv_sem.at[i],
            device_id=peer, device_id_type=MESH,
        )
        copy.start()
        sends.append(copy)
        return copy

    def own_column(ref, start, n, slot):
        row = ref[pl.ds(start // B, 1), :]
        columns[slot] = jnp.transpose(jnp.broadcast_to(row, (B, B)))
        return columns[slot, pl.ds(pl.multiple_of(start % B, n), n), :][:, :1]

    def half_of_fit(f, weight):
        fit_half[f] = (fit[f] - fit_dual[f] + weight * targets[f]) / (1.0 + weight)

    weight = [own_column(weight_ref, f * fpart + y * fseg, fseg, f) for f in range(SUBF)]
    penalty = [
        own_column(penalty_ref, u * part_rows + c * half + z * seg, seg, SUBF + u) for u in range(SUBC)
    ]
    M = 512
    stores = []

    def store(src, dst):
        copy = pltpu.make_async_copy(src, dst, store_sem.at[len(stores)])
        copy.start()
        stores.append(copy)

    for it in range(ITERS):
        last = it == ITERS - 1
        sent = {}

        def tile_part(u):
            us = pl.ds(u * part_rows, part_rows)
            back = lax.dot_general(
                design[:, u * part_rows : (u + 1) * part_rows], sb, (((0,), (0,)), ((), ())),
                preferred_element_type=F32,
            )
            tile = local[us, :] - back
            mine[it, us, :] = tile
            if not last:
                tiles[us, :] = tile
            sent["c", u] = send(mine.at[it, at(u, 1 - c, 0, 4)], from_core.at[it, u], core_peer)

        def z_reduce(u):
            sent["c", u].wait_recv()
            here = at(u, c, 0, 4)
            mine[it, here, :] = mine[it, here, :] + from_core[it, u]
            sent["z", u] = [
                send(mine.at[it, at(u, c, (z + o) % 4)], from_z.at[it, u, o - 1], z_peer[o]) for o in (2, 1, 3)
            ]

        def fit_part(f):
            sent["y", f] = [
                send(outs.at[it, fat(f, (y + o) % 4)], from_y.at[it, f, o - 1], y_peer[o]) for o in (2, 1, 3)
            ]

        def x_reduce(u):
            for copy in sent["z", u]:
                copy.wait_recv()
            here = at(u, c, z)
            to_x[it, u] = (mine[it, here, :] + from_z[it, u, 0]) + (from_z[it, u, 1] + from_z[it, u, 2])
            sent["x", u] = send(to_x.at[it, u], from_x.at[it, u], x_peer)

        def xl_reduce(f):
            for copy in sent["y", f]:
                copy.wait_recv()
            here = fat(f, y)
            to_xl[it, f] = (outs[it, here, :] + from_y[it, f, 0]) + (from_y[it, f, 1] + from_y[it, f, 2])
            sent["xl", f] = send(to_xl.at[it, f], from_xl.at[it, f], xl_peer)

        def coef_step(u):
            sent["x", u].wait_recv()
            new = (coef_half[u] + (to_x[it, u] + from_x[it, u])) / 17.0
            here = at(u, c, z)
            whole[it, here, :] = new
            sent["g", u] = [send(whole.at[it, here], whole.at[it, here], z_peer[o]) for o in (2, 1, 3)]
            if not last:
                own_dual[u] = own_dual[u] + coef_half[u] - new
                own_coef[u] = new

        def fit_step(f):
            sent["xl", f].wait_recv()
            gap = (fit_half[f] - (to_xl[it, f] + from_xl[it, f])) / 9.0
            new = fit_half[f] - gap
            here = fat(f, y)
            gaps[it, here, :] = new if last else gap
            sent["w", f] = [send(gaps.at[it, here], gaps.at[it, here], y_peer[o]) for o in (2, 1, 3)]
            if not last:
                fit_dual[f] = fit_dual[f] + fit_half[f] - new
                fit[f] = new

        def to_core(u):
            for copy in sent["g", u]:
                copy.wait_recv()
            here = at(u, c, 0, 4)
            sent["d", u] = send(whole.at[it, here], whole.at[it, here], core_peer)

        def fit_end(f):
            for copy in sent["w", f]:
                copy.wait_recv()
            fs = pl.ds(f * fpart, fpart)
            if last:
                store(gaps.at[it, fs], fit_out.at[fs])
            else:
                new = outs[it, fs, :] + gaps[it, fs, :]
                target[fs, :] = new - (part_dual[fs, :] - new)

        def coef_end(u):
            sent["d", u].wait_recv()
            us = pl.ds(u * part_rows, part_rows)
            if last:
                store(whole.at[it, us], coef_out.at[us])
            else:
                new = whole[it, us, :]
                here = new - (tile_dual[us, :] - new)
                local[us, :] = here
                lb = here.astype(BF16)
                for m in range(rows // M):
                    ms = pl.ds(m * M, M)
                    prod = dot(design[ms, u * part_rows : (u + 1) * part_rows], lb)
                    resid[ms, :] = prod if u == 0 else prod + resid[ms, :]

        if it == 0:
            for copy in first:
                copy.wait()
        else:
            resid[...] = resid[...] - target[...]
        r_hi, r_lo = split(resid[...])
        solved = []
        for m in range(rows // M):
            ms = pl.ds(m * M, M)
            s = dot(hi[ms, :], r_hi) + dot(lo[ms, :], r_hi) + dot(hi[ms, :], r_lo)
            solved.append(s.astype(BF16))
            outs[it, ms, :] = target[ms, :] + s
            if it == 0 and m == 0:
                pl.semaphore_wait(barrier, len(peers))
        sb = jnp.concatenate(solved, axis=0)
        if it == 0:
            for copy in second:
                copy.wait()
        for u in range(SUBC):
            tile_part(u)
            if u:
                z_reduce(u - 1)
            if u > 1:
                fit_part(u - 2)
        z_reduce(SUBC - 1)
        for f in range(SUBC - 2, SUBF):
            fit_part(f)
        if it == 0:
            for copy in third:
                copy.wait()
        for f in range(SUBF):
            half_of_fit(f, weight[f])
        for u in range(SUBC):
            coef_half[u] = shrink_rows(own_coef[u] - own_dual[u], penalty[u])
        if not last:
            part_dual[...] = part_dual[...] + outs[it]
            for u in range(SUBC):
                us = pl.ds(u * part_rows, part_rows)
                tile_dual[us, :] = tile_dual[us, :] + tiles[us, :]
        order = []
        stages = [
            (0, x_reduce, SUBC), (0.5, xl_reduce, SUBF), (1.7, coef_step, SUBC), (2.5, fit_step, SUBF),
            (4.0, to_core, SUBC), (5.4, fit_end, SUBF), (5.0, coef_end, SUBC),
        ]
        for offset, stage, k in stages:
            for u in range(k):
                order.append((u * 4.0 / k + offset , len(order), stage, u))
        for _, _, stage, u in sorted(order, key=lambda e: e[:2]):
            stage(u)
    for copy in sends:
        copy.wait_send()
    for copy in stores:
        copy.wait()


def iterate(
    design, hi, lo, local, target, resid, targets, weight, penalty, coef, coef_dual, tile_dual, fit, fit_dual, part_dual
):
    rows, cols = design.shape
    width = coef.shape[1]
    seg = cols // SUBC // 8
    fseg = rows // SUBF // 4
    any_ = pl.BlockSpec(memory_space=pl.ANY)
    vmem = pl.BlockSpec(memory_space=pltpu.VMEM)
    f32 = lambda *shape: pltpu.VMEM(shape + (width,), F32)
    n_copies = ITERS * (9 * SUBC + 7 * SUBF)
    return pl.pallas_call(
        iterate_kernel,
        out_shape=[jax.ShapeDtypeStruct((cols, width), F32), jax.ShapeDtypeStruct((rows, width), F32)],
        in_specs=[any_] * 7 + [vmem] * 2 + [any_] * 6,
        out_specs=[any_] * 2,
        scratch_shapes=[
            pltpu.VMEM((rows, cols), BF16), pltpu.VMEM((rows, rows), BF16), pltpu.VMEM((rows, rows), BF16),
            f32(cols), f32(SUBC, seg), f32(SUBC, seg), f32(cols), f32(SUBF, fseg), f32(SUBF, fseg), f32(SUBF, fseg),
            f32(rows), f32(rows), f32(rows), f32(SUBC, seg), f32(SUBF, fseg), pltpu.VMEM((SUBC + SUBF, B, B), F32), f32(cols),
            f32(ITERS, cols), f32(ITERS, SUBC, 4 * seg), f32(ITERS, SUBC, 3, seg),
            f32(ITERS, SUBC, seg), f32(ITERS, SUBC, seg), f32(ITERS, cols),
            f32(ITERS, rows), f32(ITERS, SUBF, 3, fseg), f32(ITERS, SUBF, fseg),
            f32(ITERS, SUBF, fseg), f32(ITERS, rows),
            pltpu.SemaphoreType.DMA((8 + 2 * SUBC + 3 * SUBF,)), pltpu.SemaphoreType.DMA((n_copies,)),
            pltpu.SemaphoreType.DMA((n_copies,)), pltpu.SemaphoreType.DMA((SUBC + SUBF,)),
        ],
        compiler_params=pltpu.CompilerParams(
            collective_id=0, has_side_effects=True, vmem_limit_bytes=VMEM_LIMIT
        ),
    )(design, hi, lo, local, target, resid, targets, weight.reshape(-1, B), penalty.reshape(-1, B), coef, coef_dual,
      tile_dual, fit, fit_dual, part_dual)


def publish_kernel(a, b, a_out, b_out, a_buf, b_buf, in_sem, out_sem):
    steps = []
    for src, buf, dst in ((a, a_buf, a_out), (b, b_buf, b_out)):
        for i in range(src.shape[0] // 512):
            rows = pl.ds(i * 512, 512)
            n = len(steps)
            steps.append((
                pltpu.make_async_copy(src.at[rows], buf.at[rows], in_sem.at[n]),
                pltpu.make_async_copy(buf.at[rows], dst.at[rows], out_sem.at[n]),
            ))
    for first, _ in steps:
        first.start()
    for first, second in steps:
        first.wait()
        second.start()
    for _, second in steps:
        second.wait()


def publish(a, b):
    any_ = pl.BlockSpec(memory_space=pl.ANY)
    n = (a.shape[0] + b.shape[0]) // 512
    return pl.pallas_call(
        publish_kernel,
        out_shape=[jax.ShapeDtypeStruct(a.shape, F32), jax.ShapeDtypeStruct(b.shape, F32)],
        in_specs=[any_] * 2,
        out_specs=[any_] * 2,
        scratch_shapes=[
            pltpu.VMEM(a.shape, F32), pltpu.VMEM(b.shape, F32), pltpu.SemaphoreType.DMA((n,)),
            pltpu.SemaphoreType.DMA((n,)),
        ],
        compiler_params=pltpu.CompilerParams(vmem_limit_bytes=VMEM_LIMIT),
    )(a, b)


def per_device(design, targets, weight, penalty, coef, coef_dual, tile_dual, fit, fit_dual, part, part_dual):
    tile_dual, part, part_dual = tile_dual[0], part[0], part_dual[0]
    hi, lo, local, target, resid = factor(design, coef, tile_dual, part, part_dual)
    coef, fit = iterate(
        design, hi, lo, local, target, resid, targets, weight, penalty, coef, coef_dual, tile_dual, fit, fit_dual, part_dual
    )
    return tuple(publish(coef, fit))


def solution(mesh):
    return jax.shard_map(
        per_device,
        mesh=mesh,
        in_specs=(
            P("smp", "feat"),
            P("smp", None),
            P("smp"),
            P("feat"),
            P("feat", None),
            P("feat", None),
            P("smp", "feat", None),
            P("smp", None),
            P("smp", None),
            P("feat", "smp", None),
            P("feat", "smp", None),
        ),
        out_specs=(P("feat", None), P("smp", None)),
        check_vma=False,
    )
```

```python
import functools
import jax
import jax.numpy as jnp
from jax import lax
from jax.experimental import pallas as pl
from jax.experimental.pallas import tpu as pltpu
from jax.sharding import PartitionSpec as P

F32, BF16 = jnp.float32, jnp.bfloat16
B = 128
NN, NT, TN = ((1,), (0,)), ((1,), (1,)), ((0,), (0,))


def split(x):
    hi = x.astype(BF16)
    return hi, (x - hi.astype(F32)).astype(BF16)


def dot(a, b, dims=NN):
    return lax.dot_general(a, b, (dims, ((), ())), preferred_element_type=F32)


def dot3(a, b, dims=NN):
    left = jnp.concatenate([a[0], a[1], a[0]], axis=dims[0][0])
    right = jnp.concatenate([b[0], b[0], b[1]], axis=dims[1][0])
    return dot(left, right, dims)


SQUARINGS = 11


def bounds():
    out = []
    target = 2.0**-13
    for _ in range(SQUARINGS):
        target = (2.0 * target / (1.0 + target)) ** 0.5
        out.append((1.0 + target) / (1.0 - target))
    return out


def leaf_inverse(s):
    n = s.shape[0]
    top = jnp.max(jnp.sum(jnp.abs(s), axis=0, keepdims=True), axis=1, keepdims=True)
    eye = lax.broadcasted_iota(jnp.int32, (n, n), 0) == lax.broadcasted_iota(jnp.int32, (n, n), 1)
    biggest = jnp.max(top)
    steps = jnp.int32(0)
    for b in bounds():
        steps = steps + (biggest > b).astype(jnp.int32)

    def scaled(_, carry):
        both, e = carry
        e2 = e * e
        c = 2.0 / (2.0 - e2)
        pair = split(both)
        prod = dot3(pair, (pair[0][n:], pair[1][n:]))
        x = c * (both[:n] + prod[:n])
        r = jnp.where(eye, 1.0 - c, 0.0) + c * prod[n:]
        return jnp.concatenate([x, r], axis=0), e2 * 0.5 * c

    start = 2.0 / (1.0 + top)
    both = jnp.concatenate([jnp.where(eye, start, 0.0), jnp.where(eye, 1.0, 0.0) - start * s], axis=0)
    both, e = lax.fori_loop(0, steps, scaled, (both, (top - 1.0) / (top + 1.0)))
    x = 2.0 / (2.0 - e * e) * (both[:n] + dot3(split(both[:n]), split(both[n:])))
    pair = split(x)
    residual = jnp.where(eye, 1.0, 0.0) - dot3(split(s), pair)
    return x + dot(pair[0], residual.astype(BF16))


def invert(g, o, n):
    a = pl.ds(o, n)
    if n == LEAF:
        g[a, a] = leaf_inverse(g[a, a])
        return
    h = n // 2
    a, b = pl.ds(o, h), pl.ds(o + h, h)
    invert(g, o, h)
    low = split(g[b, a])
    y = split(dot3(low, split(g[a, a])))
    if h == LEAF:
        g[b, b] = g[b, b] - dot3(y, low, NT)
    else:
        q = h // 2
        upper, lower = pl.ds(o + h, q), pl.ds(o + h + q, q)
        g[upper, upper] = g[upper, upper] - dot3((y[0][:q], y[1][:q]), (low[0][:q], low[1][:q]), NT)
        g[lower, b] = g[lower, b] - dot3((y[0][q:], y[1][q:]), low, NT)
    invert(g, o + h, h)
    z = dot3(split(g[b, b]), y)
    g[b, a] = -z
    g[a, b] = -jnp.transpose(z)
    g[a, a] = g[a, a] + dot3(y, split(z), TN)


LEAF = 256


def sweep(g, n):
    R = 256

    def pivot(k, _):
        near = pl.ds(pl.multiple_of(k // 8 * 8, 8), 8)
        here = lax.broadcasted_iota(jnp.int32, (8, n), 0) == k % 8
        lane = lax.broadcasted_iota(jnp.int32, (8, n), 1) == k
        row = jnp.where(here, g[near, :], 0.0)
        p = jnp.sum(jnp.sum(jnp.where(lane, row, 0.0), axis=0, keepdims=True), axis=1, keepdims=True)
        w = jnp.where(lane & here, -1.0, row) / p
        for i in range(n // R):
            rows = pl.ds(i * R, R)
            column = lax.broadcasted_iota(jnp.int32, (R, n), 1) == k
            outer = lax.dot_general(
                row[:, i * R : (i + 1) * R], w, (TN, ((), ())), precision=lax.Precision.HIGHEST,
                preferred_element_type=F32,
            )
            g[rows, :] = jnp.where(column, 0.0, g[rows, :]) - outer
        g[near, :] = jnp.where(here, w, g[near, :])
        return 0

    lax.fori_loop(0, n, pivot, 0)
    for i in range(n // R):
        rows = pl.ds(i * R, R)
        g[rows, :] = -g[rows, :]


EASY = 256.0


def factor_kernel(
    design_hbm, coef_hbm, dual_hbm, part_hbm, part_dual_hbm,
    hi_out, lo_out, local_out, target_out, resid_out,
    a_ref, coef, dual, part, part_dual, resid, hi_ref, lo_ref, g, in_sem, out_sem,
):
    n = a_ref.shape[0]
    R = 256
    loads, stores = [], []

    def load(src, dst):
        loads.append(pltpu.make_async_copy(src, dst, in_sem.at[len(loads)]))
        loads[-1].start()

    def store(src, dst):
        stores.append(pltpu.make_async_copy(src, dst, out_sem.at[len(stores)]))
        stores[-1].start()

    for i in range(n // R):
        load(design_hbm.at[pl.ds(i * R, R)], a_ref.at[pl.ds(i * R, R)])
    for src, dst in ((coef_hbm, coef), (dual_hbm, dual), (part_hbm, part), (part_dual_hbm, part_dual)):
        load(src, dst)
    for i in range(n // R):
        rows = pl.ds(i * R, R)
        loads[i].wait()
        g[rows, : (i + 1) * R] = dot(a_ref[rows, :], a_ref[: (i + 1) * R, :], NT)
    eye = jnp.where(
        lax.broadcasted_iota(jnp.int32, (B, B), 0) == lax.broadcasted_iota(jnp.int32, (B, B), 1), 1.0, 0.0
    )
    for k in range(n // B):
        at = pl.ds(k * B, B)
        g[at, at] = g[at, at] + eye
    for copy in loads[n // R :]:
        copy.wait()
    coef[...] = coef[...] - dual[...]
    store(coef, local_out)
    part[...] = part[...] - part_dual[...]
    store(part, target_out)
    cb = coef[...].astype(BF16)
    for i in range(n // 512):
        rows = pl.ds(i * 512, 512)
        resid[rows, :] = dot(a_ref[rows, :], cb) - part[rows, :]
    store(resid, resid_out)
    by_row, by_col = [], []
    for i in range(n // R):
        for j in range(i + 1):
            block = jnp.abs(g[pl.ds(i * R, R), j * R : (j + 1) * R])
            by_col.append((j, jnp.sum(block, axis=0, keepdims=True)))
            if j < i:
                by_row.append((i, block))
    most = jnp.float32(0.0)
    for i in range(n // R):
        total = sum(s for j, s in by_col if j == i)
        left = [b for j, b in by_row if j == i]
        if left:
            total = total + jnp.max(jnp.sum(sum(left), axis=1, keepdims=True), axis=0, keepdims=True)
        most = jnp.maximum(most, jnp.max(total))
    easy = most <= EASY

    @pl.when(easy)
    def _():
        invert(g, 0, n)

    @pl.when(jnp.logical_not(easy))
    def _():
        for i in range(n // R):
            for j in range(i):
                g[j * R : (j + 1) * R, i * R : (i + 1) * R] = jnp.transpose(
                    g[i * R : (i + 1) * R, j * R : (j + 1) * R]
                )
        sweep(g, n)

    for i in range(n // R):
        rows = pl.ds(i * R, R)
        hi_ref[rows, :], lo_ref[rows, :] = split(g[rows, :])
        store(hi_ref.at[rows], hi_out.at[rows])
        store(lo_ref.at[rows], lo_out.at[rows])
    for copy in stores:
        copy.wait()


def factor(design, coef, dual, part, part_dual):
    n, cols = design.shape
    width = coef.shape[1]
    any_ = pl.BlockSpec(memory_space=pl.ANY)
    square = jax.ShapeDtypeStruct((n, n), BF16)
    tall = jax.ShapeDtypeStruct((cols, width), F32)
    flat = jax.ShapeDtypeStruct((n, width), F32)
    vmem = lambda s: pltpu.VMEM(s.shape, s.dtype)
    return pl.pallas_call(
        factor_kernel,
        out_shape=[square, square, tall, flat, flat],
        in_specs=[any_] * 5,
        out_specs=[any_] * 5,
        scratch_shapes=[
            vmem(design), vmem(tall), vmem(tall), vmem(flat), vmem(flat), vmem(flat), vmem(square), vmem(square),
            pltpu.VMEM((n, n), F32), pltpu.SemaphoreType.DMA((4 + n // 256,)), pltpu.SemaphoreType.DMA((3 + n // 128,)),
        ],
        compiler_params=pltpu.CompilerParams(vmem_limit_bytes=56 * 2**20),
    )(design, coef, dual, part, part_dual)


ITERS = 2
MESH = pl.DeviceIdType.MESH
SUBC = 4
SUBF = 4
VMEM_LIMIT = 60 * 2**20


def shrink_rows(values, penalty):
    norms = jnp.sqrt(jnp.sum(values * values, axis=1, keepdims=True) + 1e-06)
    return values * (jnp.maximum(norms - penalty, 0.0) / norms)


def iterate_kernel(
    design_hbm, hi_hbm, lo_hbm, local_hbm, target_hbm, resid_hbm, targets_hbm, weight_ref, penalty_ref,
    coef_hbm, coef_dual_hbm, tile_dual_hbm, fit_hbm, fit_dual_hbm, part_dual_hbm,
    coef_out, fit_out,
    design, hi, lo, local, own_coef, own_dual, tile_dual, fit, fit_dual, targets, target, resid, part_dual,
    coef_half, fit_half, columns, tiles,
    mine, from_core, from_z, to_x, from_x, whole, outs, from_y, to_xl, from_xl, gaps,
    load_sem, send_sem, recv_sem, store_sem,
):
    rows, cols = design.shape
    smp, feat = lax.axis_index("smp"), lax.axis_index("feat")
    xh, z, c = smp // 8, (smp // 2) % 4, smp % 2
    y, xl = feat // 2, feat % 2
    core_peer = (smp + 1 - 2 * c, feat)
    z_peer = [None] + [(xh * 8 + ((z + o) % 4) * 2 + c, feat) for o in (1, 2, 3)]
    x_peer = ((smp + 8) % 16, feat)
    y_peer = [None] + [(smp, ((y + o) % 4) * 2 + xl) for o in (1, 2, 3)]
    xl_peer = (smp, feat + 1 - 2 * xl)
    peers = [core_peer, x_peer, xl_peer] + z_peer[1:] + y_peer[1:]
    barrier = pltpu.get_barrier_semaphore()
    for peer in peers:
        pl.semaphore_signal(barrier, inc=1, device_id=peer, device_id_type=MESH)

    seg = cols // SUBC // 8
    half, part_rows = 4 * seg, 8 * seg
    fseg = rows // SUBF // 4
    fpart = 4 * fseg

    def at(u, h, q, n=1):
        return pl.ds(pl.multiple_of(u * part_rows + h * half + q * seg, seg), n * seg)

    def fat(f, q):
        return pl.ds(pl.multiple_of(f * fpart + q * fseg, fseg), fseg)

    loads = []

    def load(src, dst):
        copy = pltpu.make_async_copy(src, dst, load_sem.at[len(loads)])
        copy.start()
        loads.append(copy)
        return copy

    first = [load(hi_hbm, hi), load(resid_hbm, resid), load(lo_hbm, lo), load(target_hbm, target)]
    second = [load(design_hbm, design), load(local_hbm, local)]
    third = []
    for f in range(SUBF):
        for src, dst in ((fit_hbm, fit), (fit_dual_hbm, fit_dual), (targets_hbm, targets)):
            third.append(load(src.at[fat(f, y)], dst.at[f]))
    for u in range(SUBC):
        third.append(load(coef_hbm.at[at(u, c, z)], own_coef.at[u]))
        third.append(load(coef_dual_hbm.at[at(u, c, z)], own_dual.at[u]))
    third += [load(tile_dual_hbm, tile_dual), load(part_dual_hbm, part_dual)]

    count = [0]
    sends = []

    def send(src, dst, peer):
        i = count[0]
        count[0] += 1
        copy = pltpu.make_async_remote_copy(
            src_ref=src, dst_ref=dst, send_sem=send_sem.at[i], recv_sem=recv_sem.at[i],
            device_id=peer, device_id_type=MESH,
        )
        copy.start()
        sends.append(copy)
        return copy

    def own_column(ref, start, n, slot):
        row = ref[pl.ds(start // B, 1), :]
        columns[slot] = jnp.transpose(jnp.broadcast_to(row, (B, B)))
        return columns[slot, pl.ds(pl.multiple_of(start % B, n), n), :][:, :1]

    def half_of_fit(f, weight):
        fit_half[f] = (fit[f] - fit_dual[f] + weight * targets[f]) / (1.0 + weight)

    weight = [own_column(weight_ref, f * fpart + y * fseg, fseg, f) for f in range(SUBF)]
    penalty = [
        own_column(penalty_ref, u * part_rows + c * half + z * seg, seg, SUBF + u) for u in range(SUBC)
    ]
    M = 512
    stores = []

    def store(src, dst):
        copy = pltpu.make_async_copy(src, dst, store_sem.at[len(stores)])
        copy.start()
        stores.append(copy)

    for it in range(ITERS):
        last = it == ITERS - 1
        sent = {}

        def tile_part(u):
            us = pl.ds(u * part_rows, part_rows)
            back = lax.dot_general(
                design[:, u * part_rows : (u + 1) * part_rows], sb, (((0,), (0,)), ((), ())),
                preferred_element_type=F32,
            )
            tile = local[us, :] - back
            mine[it, us, :] = tile
            if not last:
                tiles[us, :] = tile
            sent["c", u] = send(mine.at[it, at(u, 1 - c, 0, 4)], from_core.at[it, u], core_peer)

        def z_reduce(u):
            sent["c", u].wait_recv()
            here = at(u, c, 0, 4)
            mine[it, here, :] = mine[it, here, :] + from_core[it, u]
            sent["z", u] = [
                send(mine.at[it, at(u, c, (z + o) % 4)], from_z.at[it, u, o - 1], z_peer[o]) for o in (2, 1, 3)
            ]

        def fit_part(f):
            sent["y", f] = [
                send(outs.at[it, fat(f, (y + o) % 4)], from_y.at[it, f, o - 1], y_peer[o]) for o in (2, 1, 3)
            ]

        def x_reduce(u):
            for copy in sent["z", u]:
                copy.wait_recv()
            here = at(u, c, z)
            to_x[it, u] = (mine[it, here, :] + from_z[it, u, 0]) + (from_z[it, u, 1] + from_z[it, u, 2])
            sent["x", u] = send(to_x.at[it, u], from_x.at[it, u], x_peer)

        def xl_reduce(f):
            for copy in sent["y", f]:
                copy.wait_recv()
            here = fat(f, y)
            to_xl[it, f] = (outs[it, here, :] + from_y[it, f, 0]) + (from_y[it, f, 1] + from_y[it, f, 2])
            sent["xl", f] = send(to_xl.at[it, f], from_xl.at[it, f], xl_peer)

        def coef_step(u):
            sent["x", u].wait_recv()
            new = (coef_half[u] + (to_x[it, u] + from_x[it, u])) / 17.0
            here = at(u, c, z)
            whole[it, here, :] = new
            sent["g", u] = [send(whole.at[it, here], whole.at[it, here], z_peer[o]) for o in (2, 1, 3)]
            if not last:
                own_dual[u] = own_dual[u] + coef_half[u] - new
                own_coef[u] = new

        def fit_step(f):
            sent["xl", f].wait_recv()
            gap = (fit_half[f] - (to_xl[it, f] + from_xl[it, f])) / 9.0
            new = fit_half[f] - gap
            here = fat(f, y)
            gaps[it, here, :] = new if last else gap
            sent["w", f] = [send(gaps.at[it, here], gaps.at[it, here], y_peer[o]) for o in (2, 1, 3)]
            if not last:
                fit_dual[f] = fit_dual[f] + fit_half[f] - new
                fit[f] = new

        def to_core(u):
            for copy in sent["g", u]:
                copy.wait_recv()
            here = at(u, c, 0, 4)
            sent["d", u] = send(whole.at[it, here], whole.at[it, here], core_peer)

        def fit_end(f):
            for copy in sent["w", f]:
                copy.wait_recv()
            fs = pl.ds(f * fpart, fpart)
            if last:
                store(gaps.at[it, fs], fit_out.at[fs])
            else:
                new = outs[it, fs, :] + gaps[it, fs, :]
                target[fs, :] = new - (part_dual[fs, :] - new)

        def coef_end(u):
            sent["d", u].wait_recv()
            us = pl.ds(u * part_rows, part_rows)
            if last:
                store(whole.at[it, us], coef_out.at[us])
            else:
                new = whole[it, us, :]
                here = new - (tile_dual[us, :] - new)
                local[us, :] = here
                lb = here.astype(BF16)
                for m in range(rows // M):
                    ms = pl.ds(m * M, M)
                    prod = dot(design[ms, u * part_rows : (u + 1) * part_rows], lb)
                    resid[ms, :] = prod if u == 0 else prod + resid[ms, :]

        if it == 0:
            for copy in first:
                copy.wait()
        else:
            resid[...] = resid[...] - target[...]
        r_hi, r_lo = split(resid[...])
        solved = []
        for m in range(rows // M):
            ms = pl.ds(m * M, M)
            s = dot(hi[ms, :], r_hi) + dot(lo[ms, :], r_hi) + dot(hi[ms, :], r_lo)
            solved.append(s.astype(BF16))
            outs[it, ms, :] = target[ms, :] + s
            if it == 0 and m == 0:
                pl.semaphore_wait(barrier, len(peers))
        sb = jnp.concatenate(solved, axis=0)
        if it == 0:
            for copy in second:
                copy.wait()
        for u in range(SUBC):
            tile_part(u)
            if u:
                z_reduce(u - 1)
            if u > 1:
                fit_part(u - 2)
        z_reduce(SUBC - 1)
        for f in range(SUBC - 2, SUBF):
            fit_part(f)
        if it == 0:
            for copy in third:
                copy.wait()
        for f in range(SUBF):
            half_of_fit(f, weight[f])
        for u in range(SUBC):
            coef_half[u] = shrink_rows(own_coef[u] - own_dual[u], penalty[u])
        if not last:
            part_dual[...] = part_dual[...] + outs[it]
            for u in range(SUBC):
                us = pl.ds(u * part_rows, part_rows)
                tile_dual[us, :] = tile_dual[us, :] + tiles[us, :]
        order = []
        stages = [
            (0, x_reduce, SUBC), (0.5, xl_reduce, SUBF), (1.7, coef_step, SUBC), (2.5, fit_step, SUBF),
            (4.0, to_core, SUBC), (5.4, fit_end, SUBF), (5.0, coef_end, SUBC),
        ]
        for offset, stage, k in stages:
            for u in range(k):
                order.append((u * 4.0 / k + offset , len(order), stage, u))
        for _, _, stage, u in sorted(order, key=lambda e: e[:2]):
            stage(u)
    for copy in sends:
        copy.wait_send()
    for copy in stores:
        copy.wait()


def iterate(
    design, hi, lo, local, target, resid, targets, weight, penalty, coef, coef_dual, tile_dual, fit, fit_dual, part_dual
):
    rows, cols = design.shape
    width = coef.shape[1]
    seg = cols // SUBC // 8
    fseg = rows // SUBF // 4
    any_ = pl.BlockSpec(memory_space=pl.ANY)
    vmem = pl.BlockSpec(memory_space=pltpu.VMEM)
    f32 = lambda *shape: pltpu.VMEM(shape + (width,), F32)
    n_copies = ITERS * (9 * SUBC + 7 * SUBF)
    return pl.pallas_call(
        iterate_kernel,
        out_shape=[jax.ShapeDtypeStruct((cols, width), F32), jax.ShapeDtypeStruct((rows, width), F32)],
        in_specs=[any_] * 7 + [vmem] * 2 + [any_] * 6,
        out_specs=[any_] * 2,
        scratch_shapes=[
            pltpu.VMEM((rows, cols), BF16), pltpu.VMEM((rows, rows), BF16), pltpu.VMEM((rows, rows), BF16),
            f32(cols), f32(SUBC, seg), f32(SUBC, seg), f32(cols), f32(SUBF, fseg), f32(SUBF, fseg), f32(SUBF, fseg),
            f32(rows), f32(rows), f32(rows), f32(SUBC, seg), f32(SUBF, fseg), pltpu.VMEM((SUBC + SUBF, B, B), F32), f32(cols),
            f32(ITERS, cols), f32(ITERS, SUBC, 4 * seg), f32(ITERS, SUBC, 3, seg),
            f32(ITERS, SUBC, seg), f32(ITERS, SUBC, seg), f32(ITERS, cols),
            f32(ITERS, rows), f32(ITERS, SUBF, 3, fseg), f32(ITERS, SUBF, fseg),
            f32(ITERS, SUBF, fseg), f32(ITERS, rows),
            pltpu.SemaphoreType.DMA((8 + 2 * SUBC + 3 * SUBF,)), pltpu.SemaphoreType.DMA((n_copies,)),
            pltpu.SemaphoreType.DMA((n_copies,)), pltpu.SemaphoreType.DMA((SUBC + SUBF,)),
        ],
        compiler_params=pltpu.CompilerParams(
            collective_id=0, has_side_effects=True, vmem_limit_bytes=VMEM_LIMIT
        ),
    )(design, hi, lo, local, target, resid, targets, weight.reshape(-1, B), penalty.reshape(-1, B), coef, coef_dual,
      tile_dual, fit, fit_dual, part_dual)


def publish_kernel(a, b, a_out, b_out, a_buf, b_buf, in_sem, out_sem):
    steps = []
    for src, buf, dst in ((a, a_buf, a_out), (b, b_buf, b_out)):
        for i in range(src.shape[0] // 512):
            rows = pl.ds(i * 512, 512)
            n = len(steps)
            steps.append((
                pltpu.make_async_copy(src.at[rows], buf.at[rows], in_sem.at[n]),
                pltpu.make_async_copy(buf.at[rows], dst.at[rows], out_sem.at[n]),
            ))
    for first, _ in steps:
        first.start()
    for first, second in steps:
        first.wait()
        second.start()
    for _, second in steps:
        second.wait()


def publish(a, b):
    any_ = pl.BlockSpec(memory_space=pl.ANY)
    n = (a.shape[0] + b.shape[0]) // 512
    return pl.pallas_call(
        publish_kernel,
        out_shape=[jax.ShapeDtypeStruct(a.shape, F32), jax.ShapeDtypeStruct(b.shape, F32)],
        in_specs=[any_] * 2,
        out_specs=[any_] * 2,
        scratch_shapes=[
            pltpu.VMEM(a.shape, F32), pltpu.VMEM(b.shape, F32), pltpu.SemaphoreType.DMA((n,)),
            pltpu.SemaphoreType.DMA((n,)),
        ],
        compiler_params=pltpu.CompilerParams(vmem_limit_bytes=VMEM_LIMIT),
    )(a, b)


def per_device(design, targets, weight, penalty, coef, coef_dual, tile_dual, fit, fit_dual, part, part_dual):
    tile_dual, part, part_dual = tile_dual[0], part[0], part_dual[0]
    hi, lo, local, target, resid = factor(design, coef, tile_dual, part, part_dual)
    coef, fit = iterate(
        design, hi, lo, local, target, resid, targets, weight, penalty, coef, coef_dual, tile_dual, fit, fit_dual, part_dual
    )
    return tuple(publish(coef, fit))


def solution(mesh):
    return jax.shard_map(
        per_device,
        mesh=mesh,
        in_specs=(
            P("smp", "feat"),
            P("smp", None),
            P("smp"),
            P("feat"),
            P("feat", None),
            P("feat", None),
            P("smp", "feat", None),
            P("smp", None),
            P("smp", None),
            P("feat", "smp", None),
            P("feat", "smp", None),
        ),
        out_specs=(P("feat", None), P("smp", None)),
        check_vma=False,
    )
```
